256 devices in a mesh: beam: 32 (over x, y, core), tensor: 8 (over z).
Axes of the slice: x: 4, y: 4, z: 8, core: 2. Of those that a mesh axis runs over, the one named last changes fastest.
Arguments:
- parents: int32 [256], P('beam'), may hold values from 0 to 255, as said below
- lengths: int32 [256], P('beam'), may hold values from 256 to 2048
- queries: bfloat16 [256, 8192], P('beam', 'tensor'), may hold values from -8 to 8
- token_keys: bfloat16 [256, 1024], P('beam', 'tensor'), may hold values from -6 to 6
- token_values: bfloat16 [256, 1024], P('beam', 'tensor'), may hold values from -6 to 6
- key_cache: bfloat16 [256, 8, 2048, 128], P('beam', 'tensor'), may hold values from -3 to 3
- cached_value_rows: bfloat16 [256, 8, 2048, 128], P('beam', 'tensor'), may hold values from -6 to 6
- output_weight: bfloat16 [8192, 8192], P('tensor', 'beam'), may hold values from -0.0625 to 0.0625
Outputs:
- projected: bfloat16 [256, 8192], P('tensor', 'beam')
The draws below stay inside these ranges and needn't reach their ends.
Inputs may be any that keep to these rules, and one draw needn't show every extreme that they name: The parent of a new slot is one of the 32 old slots of the same query. In each aligned block of 8 new slots, exactly 2 parents lie in each aligned block of 8 old slots of that query when 8 * 8 >= 32, else at most one does.
All inputs are finite; a program needn't handle non-finite values.
Results may differ from the reference program's by a relative error of at most 0.0056.
Values may be sent and summed in bfloat16 or wider, within the bound.
No kernel may reach another device: no remote copies, remote signals or barrier semaphores. Data moves between devices by JAX's collectives and lax.ppermute only.
A program may use at most 128 MiB of HBM per device.

```python
import jax
import jax.numpy as jnp
from jax import lax

D = 8192
QUERY_HEADS = 64
KEY_VALUE_HEADS = 8
HEAD_SIZE = 128
CACHE_POSITIONS = 2048
BEAMS = 32
SLOT_DEV = 8
TOTAL_SLOTS = 256


def draw_queries(key, part):
    key = jax.random.fold_in(key, 1)
    key_base = jax.random.fold_in(key, 0)
    base_offset = jnp.clip(jax.random.normal(key_base, (TOTAL_SLOTS, QUERY_HEADS, HEAD_SIZE), jnp.float32), -8.0, 8.0)
    return base_offset.reshape(TOTAL_SLOTS, QUERY_HEADS * HEAD_SIZE).astype(jnp.bfloat16)


def draw_key_cache(key, part):
    key = jax.random.fold_in(key, 2)
    base_offset = jnp.clip(jax.random.normal(key, (TOTAL_SLOTS, KEY_VALUE_HEADS, CACHE_POSITIONS, HEAD_SIZE), jnp.float32), -3.0, 3.0)
    return base_offset.astype(jnp.bfloat16)


def draw_lengths(key, part):
    key = jax.random.fold_in(key, 3)
    key_base, key_extra = jax.random.split(key, 2)
    base_offset = jax.random.randint(key_base, (TOTAL_SLOTS // BEAMS,), CACHE_POSITIONS // 8, CACHE_POSITIONS - CACHE_POSITIONS // 16 + 1)
    extra = jax.random.randint(key_extra, (TOTAL_SLOTS,), 0, CACHE_POSITIONS // 16 + 1)
    slot_ids = jnp.arange(TOTAL_SLOTS)
    result = base_offset[slot_ids // BEAMS] + extra
    return jnp.where(slot_ids == 0, CACHE_POSITIONS, result).astype(jnp.int32)


def draw_parents(key, part):
    key = jax.random.fold_in(key, 4)
    key_order, key_shift, key_local = jax.random.split(key, 3)
    group_size = BEAMS // SLOT_DEV
    blocks = TOTAL_SLOTS // SLOT_DEV
    scores = jax.random.randint(key_order, (blocks, SLOT_DEV), 0, 1 << 20) * SLOT_DEV + jnp.arange(SLOT_DEV)[None, :]
    ranking = jnp.argsort(scores, axis=1).astype(jnp.int32)
    shift_by = jax.random.randint(key_shift, (blocks, 1), 0, group_size)
    source_pos = (ranking + shift_by) % group_size
    local_row = jax.random.randint(key_local, (blocks, SLOT_DEV), 0, SLOT_DEV)
    slot_ids = jnp.arange(TOTAL_SLOTS).reshape(blocks, SLOT_DEV)
    parent = slot_ids // BEAMS * BEAMS + source_pos * SLOT_DEV + local_row
    return parent.reshape(TOTAL_SLOTS).astype(jnp.int32)


def block_scale(stream_key, extent, cuts, smallest, top_value):
    level = 1.0
    for dim, blocks in cuts:
        heights = jax.random.uniform(jax.random.fold_in(jax.random.fold_in(stream_key, 6), dim), (blocks,), jnp.float32, smallest / len(cuts), top_value / len(cuts))
        level = level * jnp.repeat(jnp.exp(heights), extent[dim] // blocks).reshape((-1,) + (1,) * (len(extent) - 1 - dim))
    return level


def normal_values(stream_key, dims, spread, bound, cuts=(), kind=jnp.bfloat16):
    level = block_scale(stream_key, dims, cuts, -0.22, 0.18) if cuts else 1.0
    values = jax.random.normal(stream_key, dims, jnp.float32) * spread * level
    return jnp.minimum(jnp.maximum(values, -bound), bound).astype(kind)


def setup_inputs(seed: int = 0) -> dict:
    arg_keys = jax.random.split(jax.random.key(seed), 9)
    parents = draw_parents(jax.random.fold_in(arg_keys[8], 71), 0)
    lengths = draw_lengths(jax.random.fold_in(arg_keys[8], 71), 0)
    queries = draw_queries(jax.random.fold_in(arg_keys[8], 71), 0)
    token_keys = normal_values(arg_keys[3], (TOTAL_SLOTS, KEY_VALUE_HEADS * HEAD_SIZE), 1.0, 6.0, ((0, 32), (1, 8)))
    token_values = normal_values(arg_keys[4], (TOTAL_SLOTS, KEY_VALUE_HEADS * HEAD_SIZE), 1.0, 6.0, ((0, 32), (1, 8)))
    key_cache = draw_key_cache(jax.random.fold_in(arg_keys[8], 71), 0)
    cached_value_rows = normal_values(arg_keys[6], (TOTAL_SLOTS, KEY_VALUE_HEADS, CACHE_POSITIONS, HEAD_SIZE), 1.0, 6.0, ((0, 32), (1, 8)))
    output_weight = normal_values(arg_keys[7], (QUERY_HEADS * HEAD_SIZE, D), (QUERY_HEADS * HEAD_SIZE) ** -0.5, 0.0625, ((0, 8), (1, 32)))
    return {"parents": parents, "lengths": lengths, "queries": queries, "token_keys": token_keys, "token_values": token_values, "key_cache": key_cache, "cached_value_rows": cached_value_rows, "output_weight": output_weight}


def reference(parents, lengths, queries, token_keys, token_values, key_cache, cached_value_rows, output_weight):
    score_scale = HEAD_SIZE ** -0.5
    grouped_queries = QUERY_HEADS // KEY_VALUE_HEADS

    def one_slot(slot_number):
        parent = parents[slot_number]
        key_rows = lax.dynamic_index_in_dim(key_cache, parent, 0, keepdims=False).astype(jnp.float32)
        value_rows = lax.dynamic_index_in_dim(cached_value_rows, parent, 0, keepdims=False).astype(jnp.float32)
        length = lengths[parent]
        query_head_rows = lax.dynamic_index_in_dim(queries, slot_number, 0, keepdims=False).reshape(KEY_VALUE_HEADS, grouped_queries, HEAD_SIZE).astype(jnp.float32)
        fresh_key = lax.dynamic_index_in_dim(token_keys, slot_number, 0, keepdims=False).reshape(KEY_VALUE_HEADS, HEAD_SIZE).astype(jnp.float32)
        fresh_value = lax.dynamic_index_in_dim(token_values, slot_number, 0, keepdims=False).reshape(KEY_VALUE_HEADS, HEAD_SIZE).astype(jnp.float32)
        scores = jnp.einsum('kgd,kld->kgl', query_head_rows, key_rows) * score_scale
        valid = jnp.arange(CACHE_POSITIONS, dtype=jnp.int32) < length
        scores = jnp.where(valid[None, None, :], scores, -1e30)
        new_score = jnp.einsum('kgd,kd->kg', query_head_rows, fresh_key) * score_scale
        maximum = jnp.maximum(jnp.max(scores, axis=-1), new_score)
        weights = jnp.exp(scores - maximum[..., None])
        new_weight = jnp.exp(new_score - maximum)
        denominator = jnp.sum(weights, axis=-1) + new_weight
        rounded = lax.optimization_barrier(weights.astype(jnp.bfloat16)).astype(jnp.float32)
        rounded_new = lax.optimization_barrier(new_weight.astype(jnp.bfloat16)).astype(jnp.float32)
        weighted = jnp.einsum('kgl,kld->kgd', rounded, value_rows) + rounded_new[..., None] * fresh_value[:, None, :]
        return (weighted / denominator[..., None]).astype(jnp.bfloat16).reshape(QUERY_HEADS * HEAD_SIZE)

    heads_out = lax.map(one_slot, jnp.arange(TOTAL_SLOTS, dtype=jnp.int32))
    return jnp.dot(heads_out, output_weight, preferred_element_type=jnp.float32).astype(jnp.bfloat16)
```

```python
import jax
import jax.numpy as jnp
from jax import lax
from jax.experimental import pallas as pl
from jax.experimental.pallas import tpu as pltpu
from jax.sharding import Mesh
from jax.sharding import PartitionSpec as P

HEAD = 128
GROUPED = 8
SLOTS = 8
BEAMS = 32
POSITIONS = 2048
Q_COLS = GROUPED * HEAD
IN_COLS = Q_COLS + 3 * HEAD
OUT_COLS = Q_COLS + HEAD
BEAM_AXES = ("x", "y", "core")
F32 = jnp.float32
BF16 = jnp.bfloat16
VMEM = pl.BlockSpec(memory_space=pltpu.VMEM)
SMEM = pl.BlockSpec(memory_space=pltpu.SMEM)


def beam_index():
    return (lax.axis_index("x") * 4 + lax.axis_index("y")) * 2 + lax.axis_index("core")


def transposed_dot(a, b):
    return lax.dot_general(a, b, (((0,), (0,)), ((), ())), preferred_element_type=F32)


def attend_kernel(len_ref, m0, m1, m2, m3, k_ref, v_ref, out_ref, q_ref, s_ref, o_ref):
    own = beam_index()
    member = own % 4
    rows = lax.broadcasted_iota(jnp.int32, (BEAMS, HEAD), 0)
    lanes = lax.broadcasted_iota(jnp.int32, (BEAMS, HEAD), 1)
    slot_ids = ((member ^ (rows // SLOTS)) * SLOTS + rows % SLOTS).astype(F32)
    everything = jnp.concatenate([m[...].astype(F32) for m in (m0, m1, m2, m3)], axis=0)
    parents = everything[:, IN_COLS - HEAD :].astype(jnp.int32)
    local = (parents // SLOTS) == own
    before = (
        lax.broadcasted_iota(jnp.int32, (BEAMS, BEAMS), 1)
        < lax.broadcasted_iota(jnp.int32, (BEAMS, BEAMS), 0)
    )
    rank = jnp.dot(
        before.astype(F32).astype(BF16), local.astype(F32).astype(BF16), preferred_element_type=F32
    ).astype(jnp.int32)
    pick = (local & (rank == lanes)).astype(F32).astype(BF16)
    wide = jnp.concatenate([everything, slot_ids], axis=1).astype(BF16)
    chosen = transposed_dot(pick, wide)[:SLOTS]
    fresh_keys = chosen[:, Q_COLS : Q_COLS + HEAD]
    fresh_values = chosen[:, Q_COLS + HEAD : Q_COLS + 2 * HEAD]
    cache_rows = chosen[:, Q_COLS + 2 * HEAD : IN_COLS].astype(jnp.int32) - own * SLOTS
    ids = chosen[:, IN_COLS:]
    for h in range(GROUPED):
        q_ref[h * SLOTS : (h + 1) * SLOTS, :] = chosen[:, h * HEAD : (h + 1) * HEAD]
    scale = HEAD ** (-0.5)
    positions = lax.broadcasted_iota(jnp.int32, (GROUPED, POSITIONS), 1)
    picked, new_scores = [], []
    for i in range(SLOTS):
        row = jnp.clip(cache_rows[i, 0], 0, SLOTS - 1)
        picked.append(row)
        q = q_ref[pl.ds(i, GROUPED, stride=SLOTS), :]
        scores = lax.dot_general(
            q.astype(BF16), k_ref[row], (((1,), (1,)), ((), ())), preferred_element_type=F32
        ) * scale
        s_ref[i] = jnp.where(positions < len_ref[row], scores, -1e30)
        new_scores.append(jnp.sum(q * fresh_keys[i : i + 1], axis=1, keepdims=True) * scale)
    for i in range(SLOTS):
        scores = s_ref[i]
        maximum = jnp.maximum(jnp.max(scores, axis=1, keepdims=True), new_scores[i])
        weights = jnp.exp(scores - maximum)
        new_weight = jnp.exp(new_scores[i] - maximum)
        denominator = jnp.sum(weights, axis=1, keepdims=True) + new_weight
        weighted = jnp.dot(weights.astype(BF16), v_ref[picked[i]], preferred_element_type=F32)
        weighted = weighted + new_weight.astype(BF16).astype(F32) * fresh_values[i : i + 1]
        o_ref[pl.ds(i, GROUPED, stride=SLOTS), :] = weighted / denominator
    block = jnp.concatenate(
        [o_ref[h * SLOTS : (h + 1) * SLOTS, :] for h in range(GROUPED)] + [ids], axis=1
    )
    pair = jnp.concatenate([block, block], axis=0).astype(BF16)
    for j in range(8):
        out_ref[j * 16 : (j + 1) * 16, :] = pair


def project_kernel(own_ref, other_ref, w_ref, out_ref, place_ref):
    weight = w_ref[...]
    for part, ref in enumerate((own_ref, other_ref)):
        terms = jnp.dot(ref[:, :Q_COLS], weight, preferred_element_type=F32).astype(BF16)
        for g in range(8):
            out_ref[g * 32 + part * 16 : g * 32 + part * 16 + 16, :] = terms[g * 16 : g * 16 + 16]
    first = pl.multiple_of(lax.axis_index("tensor") * 16, 16)
    lanes = lax.broadcasted_iota(jnp.int32, (16, HEAD), 1)
    for part, ref in enumerate((own_ref, other_ref)):
        ids = ref[pl.ds(first, 16), Q_COLS:].astype(F32).astype(jnp.int32)
        place_ref[part * 16 : part * 16 + 16, :] = (ids == lanes).astype(F32).astype(BF16)


def finish_kernel(terms_ref, place_ref, out_ref):
    total = terms_ref[0:32, :].astype(F32)
    for z in range(1, 8):
        total = total + terms_ref[z * 32 : z * 32 + 32, :].astype(F32)
    out_ref[...] = transposed_dot(place_ref[...], total.astype(BF16))[:BEAMS].astype(BF16)


def body(parents, lengths, queries, token_keys, token_values, key_cache, value_cache, weight):
    marks = jnp.broadcast_to(parents.astype(BF16)[:, None], (SLOTS, HEAD))
    message = jnp.concatenate([queries, token_keys, token_values, marks], axis=1)
    partners = [
        lax.ppermute(message, BEAM_AXES, [(i, i ^ d) for i in range(32)]) for d in (1, 2, 3)
    ]
    heads = pl.pallas_call(
        attend_kernel,
        out_shape=jax.ShapeDtypeStruct((16 * SLOTS, OUT_COLS), BF16),
        in_specs=[SMEM] + [VMEM] * 6,
        out_specs=VMEM,
        scratch_shapes=[
            pltpu.VMEM((GROUPED * SLOTS, HEAD), F32),
            pltpu.VMEM((SLOTS, GROUPED, POSITIONS), F32),
            pltpu.VMEM((GROUPED * SLOTS, HEAD), F32),
        ],
        compiler_params=pltpu.CompilerParams(vmem_limit_bytes=24 * 1024 * 1024),
        cost_estimate=pl.CostEstimate(
            flops=2 * 2 * 64 * 2048 * 128, bytes_accessed=9 * 2**20, transcendentals=64 * 2048
        ),
        name="attend",
    )(
        lengths,
        message,
        *partners,
        key_cache.reshape(SLOTS, POSITIONS, HEAD),
        value_cache.reshape(SLOTS, POSITIONS, HEAD),
    )
    gathered = lax.all_to_all(heads, ("x", "y"), 0, 0, tiled=True)
    other = lax.ppermute(gathered, BEAM_AXES, [(i, i ^ 1) for i in range(32)])
    terms, place = pl.pallas_call(
        project_kernel,
        out_shape=(
            jax.ShapeDtypeStruct((256, 256), BF16),
            jax.ShapeDtypeStruct((BEAMS, HEAD), BF16),
        ),
        in_specs=[VMEM] * 3,
        out_specs=(VMEM, VMEM),
        compiler_params=pltpu.CompilerParams(vmem_limit_bytes=16 * 1024 * 1024),
        name="project",
    )(gathered, other, weight)
    shares = lax.all_to_all(terms, "tensor", 0, 0, tiled=True)
    return pl.pallas_call(
        finish_kernel,
        out_shape=jax.ShapeDtypeStruct((BEAMS, 256), BF16),
        in_specs=[VMEM] * 2,
        out_specs=VMEM,
        compiler_params=pltpu.CompilerParams(vmem_limit_bytes=16 * 1024 * 1024),
        name="finish",
    )(shares, place)


def solution(mesh):
    fine = Mesh(mesh.devices.reshape(4, 4, 2, 8), ("x", "y", "core", "tensor"))
    in_specs = (
        P(BEAM_AXES),
        P(BEAM_AXES),
        P(BEAM_AXES, "tensor"),
        P(BEAM_AXES, "tensor"),
        P(BEAM_AXES, "tensor"),
        P(BEAM_AXES, "tensor", None, None),
        P(BEAM_AXES, "tensor", None, None),
        P("tensor", BEAM_AXES),
    )
    out_specs = P("tensor", BEAM_AXES)
    return jax.shard_map(body, mesh=fine, in_specs=in_specs, out_specs=out_specs, check_vma=False)
```

```python
import jax
import jax.numpy as jnp
from jax import lax
from jax.experimental import pallas as pl
from jax.experimental.pallas import tpu as pltpu
from jax.sharding import Mesh
from jax.sharding import PartitionSpec as P

HEAD = 128
GROUPED = 8
SLOTS = 8
BEAMS = 32
POSITIONS = 2048
Q_COLS = GROUPED * HEAD
IN_COLS = Q_COLS + 3 * HEAD
OUT_COLS = Q_COLS + HEAD
BEAM_AXES = ("x", "y", "core")
F32 = jnp.float32
BF16 = jnp.bfloat16
VMEM = pl.BlockSpec(memory_space=pltpu.VMEM)
HBM = pl.BlockSpec(memory_space=pltpu.HBM)


def in_hbm(x):
    return pltpu.with_memory_space_constraint(x, pltpu.HBM)


def beam_index():
    return (lax.axis_index("x") * 4 + lax.axis_index("y")) * 2 + lax.axis_index("core")


def transposed_dot(a, b):
    return lax.dot_general(a, b, (((0,), (0,)), ((), ())), preferred_element_type=F32)


def pack_kernel(parent_hbm, q_hbm, key_hbm, value_hbm, out_ref, parent_ref, sems):
    copies = [pltpu.make_async_copy(parent_hbm, parent_ref, sems.at[0])]
    start = 0
    for n, ref in enumerate((q_hbm, key_hbm, value_hbm)):
        columns = out_ref.at[:, start : start + ref.shape[1]]
        copies.append(pltpu.make_async_copy(ref, columns, sems.at[n + 1]))
        start += ref.shape[1]
    for copy in copies:
        copy.start()
    rows = lax.broadcasted_iota(jnp.int32, (SLOTS, HEAD), 0)
    marks = jnp.zeros((SLOTS, HEAD), jnp.int32)
    copies[0].wait()
    for i in range(SLOTS):
        marks = jnp.where(rows == i, parent_ref[i], marks)
    out_ref[:, start:] = marks.astype(F32).astype(BF16)
    for copy in copies[1:]:
        copy.wait()


def load_kernel(after_ref, len_hbm, k_hbm, v_hbm, k_out, v_out, len_out, len_ref, sems):
    copies = [
        pltpu.make_async_copy(len_hbm, len_ref, sems.at[0]),
        pltpu.make_async_copy(k_hbm, k_out, sems.at[1]),
        pltpu.make_async_copy(v_hbm, v_out, sems.at[2]),
    ]
    for copy in copies:
        copy.start()
    rows = lax.broadcasted_iota(jnp.int32, (SLOTS, HEAD), 0)
    spread = jnp.zeros((SLOTS, HEAD), jnp.int32)
    copies[0].wait()
    for i in range(SLOTS):
        spread = jnp.where(rows == i, len_ref[i], spread)
    len_out[...] = spread
    for copy in copies[1:]:
        copy.wait()


def attend_kernel(len_ref, m0, m1, m2, m3, k_ref, v_ref, out_ref, q_ref, s_ref, o_ref):
    own = beam_index()
    member = own % 4
    rows = lax.broadcasted_iota(jnp.int32, (BEAMS, HEAD), 0)
    lanes = lax.broadcasted_iota(jnp.int32, (BEAMS, HEAD), 1)
    slot_ids = ((member ^ (rows // SLOTS)) * SLOTS + rows % SLOTS).astype(F32)
    everything = jnp.concatenate([m[...].astype(F32) for m in (m0, m1, m2, m3)], axis=0)
    parents = everything[:, IN_COLS - HEAD :].astype(jnp.int32)
    local = (parents // SLOTS) == own
    before = (
        lax.broadcasted_iota(jnp.int32, (BEAMS, BEAMS), 1)
        < lax.broadcasted_iota(jnp.int32, (BEAMS, BEAMS), 0)
    )
    rank = jnp.dot(
        before.astype(F32).astype(BF16), local.astype(F32).astype(BF16), preferred_element_type=F32
    ).astype(jnp.int32)
    pick = (local & (rank == lanes)).astype(F32).astype(BF16)
    wide = jnp.concatenate([everything, slot_ids], axis=1).astype(BF16)
    chosen = transposed_dot(pick, wide)[:SLOTS]
    fresh_keys = chosen[:, Q_COLS : Q_COLS + HEAD]
    fresh_values = chosen[:, Q_COLS + HEAD : Q_COLS + 2 * HEAD]
    cache_rows = chosen[:, Q_COLS + 2 * HEAD : IN_COLS].astype(jnp.int32) - own * SLOTS
    ids = chosen[:, IN_COLS:]
    limits = jnp.zeros((SLOTS, HEAD), jnp.int32)
    for r in range(SLOTS):
        limits = jnp.where(cache_rows == r, len_ref[r : r + 1, :], limits)
    for h in range(GROUPED):
        q_ref[h * SLOTS : (h + 1) * SLOTS, :] = chosen[:, h * HEAD : (h + 1) * HEAD]
    scale = HEAD ** (-0.5)
    positions = lax.broadcasted_iota(jnp.int32, (GROUPED, POSITIONS), 1)
    picked, new_scores = [], []
    for i in range(SLOTS):
        row = jnp.clip(cache_rows[i, 0], 0, SLOTS - 1)
        picked.append(row)
        q = q_ref[pl.ds(i, GROUPED, stride=SLOTS), :]
        scores = lax.dot_general(
            q.astype(BF16), k_ref[row], (((1,), (1,)), ((), ())), preferred_element_type=F32
        ) * scale
        s_ref[i] = jnp.where(positions < limits[i : i + 1, :1], scores, -1e30)
        new_scores.append(jnp.sum(q * fresh_keys[i : i + 1], axis=1, keepdims=True) * scale)
    for i in range(SLOTS):
        scores = s_ref[i]
        maximum = jnp.maximum(jnp.max(scores, axis=1, keepdims=True), new_scores[i])
        weights = jnp.exp(scores - maximum)
        new_weight = jnp.exp(new_scores[i] - maximum)
        denominator = jnp.sum(weights, axis=1, keepdims=True) + new_weight
        weighted = jnp.dot(weights.astype(BF16), v_ref[picked[i]], preferred_element_type=F32)
        weighted = weighted + new_weight.astype(BF16).astype(F32) * fresh_values[i : i + 1]
        o_ref[pl.ds(i, GROUPED, stride=SLOTS), :] = weighted / denominator
    block = jnp.concatenate(
        [o_ref[h * SLOTS : (h + 1) * SLOTS, :] for h in range(GROUPED)] + [ids], axis=1
    )
    pair = jnp.concatenate([block, block], axis=0).astype(BF16)
    for j in range(8):
        out_ref[j * 16 : (j + 1) * 16, :] = pair


def project_kernel(own_ref, other_ref, w_ref, out_ref, place_ref):
    weight = w_ref[...]
    for part, ref in enumerate((own_ref, other_ref)):
        terms = jnp.dot(ref[:, :Q_COLS], weight, preferred_element_type=F32).astype(BF16)
        for g in range(8):
            out_ref[g * 32 + part * 16 : g * 32 + part * 16 + 16, :] = terms[g * 16 : g * 16 + 16]
    first = pl.multiple_of(lax.axis_index("tensor") * 16, 16)
    lanes = lax.broadcasted_iota(jnp.int32, (16, HEAD), 1)
    for part, ref in enumerate((own_ref, other_ref)):
        ids = ref[pl.ds(first, 16), Q_COLS:].astype(F32).astype(jnp.int32)
        place_ref[part * 16 : part * 16 + 16, :] = (ids == lanes).astype(F32).astype(BF16)


def finish_kernel(terms_ref, place_ref, out_ref):
    total = terms_ref[0:32, :].astype(F32)
    for z in range(1, 8):
        total = total + terms_ref[z * 32 : z * 32 + 32, :].astype(F32)
    out_ref[...] = transposed_dot(place_ref[...], total.astype(BF16))[:BEAMS].astype(BF16)


def body(parents, lengths, queries, token_keys, token_values, key_cache, value_cache, weight):
    message = pl.pallas_call(
        pack_kernel,
        out_shape=pltpu.VMEM((SLOTS, IN_COLS), BF16),
        in_specs=[HBM] * 4,
        out_specs=VMEM,
        scratch_shapes=[pltpu.SMEM((SLOTS,), jnp.int32), pltpu.SemaphoreType.DMA((4,))],
        name="pack",
    )(*[in_hbm(x) for x in (parents, queries, token_keys, token_values)])
    partners = [
        lax.ppermute(message, BEAM_AXES, [(i, i ^ d) for i in range(32)]) for d in (1, 2, 3)
    ]
    cache = pltpu.VMEM((SLOTS, POSITIONS, HEAD), BF16)
    keys, values, limits = pl.pallas_call(
        load_kernel,
        out_shape=(cache, cache, pltpu.VMEM((SLOTS, HEAD), jnp.int32)),
        in_specs=[VMEM] + [HBM] * 3,
        out_specs=(VMEM, VMEM, VMEM),
        scratch_shapes=[pltpu.SMEM((SLOTS,), jnp.int32), pltpu.SemaphoreType.DMA((3,))],
        compiler_params=pltpu.CompilerParams(vmem_limit_bytes=8 * 1024 * 1024),
        cost_estimate=pl.CostEstimate(flops=0, bytes_accessed=16 * 2**20, transcendentals=0),
        name="load",
    )(
        message,
        in_hbm(lengths),
        in_hbm(key_cache.reshape(SLOTS, POSITIONS, HEAD)),
        in_hbm(value_cache.reshape(SLOTS, POSITIONS, HEAD)),
    )
    heads = pl.pallas_call(
        attend_kernel,
        out_shape=jax.ShapeDtypeStruct((16 * SLOTS, OUT_COLS), BF16),
        in_specs=[VMEM] * 7,
        out_specs=VMEM,
        scratch_shapes=[
            pltpu.VMEM((GROUPED * SLOTS, HEAD), F32),
            pltpu.VMEM((SLOTS, GROUPED, POSITIONS), F32),
            pltpu.VMEM((GROUPED * SLOTS, HEAD), F32),
        ],
        compiler_params=pltpu.CompilerParams(vmem_limit_bytes=24 * 1024 * 1024),
        cost_estimate=pl.CostEstimate(
            flops=2 * 2 * 64 * 2048 * 128, bytes_accessed=9 * 2**20, transcendentals=64 * 2048
        ),
        name="attend",
    )(
        limits,
        message,
        *partners,
        keys,
        values,
    )
    gathered = lax.all_to_all(heads, ("x", "y"), 0, 0, tiled=True)
    other = lax.ppermute(gathered, BEAM_AXES, [(i, i ^ 1) for i in range(32)])
    terms, place = pl.pallas_call(
        project_kernel,
        out_shape=(
            jax.ShapeDtypeStruct((256, 256), BF16),
            jax.ShapeDtypeStruct((BEAMS, HEAD), BF16),
        ),
        in_specs=[VMEM] * 3,
        out_specs=(VMEM, VMEM),
        compiler_params=pltpu.CompilerParams(vmem_limit_bytes=16 * 1024 * 1024),
        name="project",
    )(gathered, other, weight)
    shares = lax.all_to_all(terms, "tensor", 0, 0, tiled=True)
    return pl.pallas_call(
        finish_kernel,
        out_shape=jax.ShapeDtypeStruct((BEAMS, 256), BF16),
        in_specs=[VMEM] * 2,
        out_specs=VMEM,
        compiler_params=pltpu.CompilerParams(vmem_limit_bytes=16 * 1024 * 1024),
        name="finish",
    )(shares, place)


def solution(mesh):
    fine = Mesh(mesh.devices.reshape(4, 4, 2, 8), ("x", "y", "core", "tensor"))
    in_specs = (
        P(BEAM_AXES),
        P(BEAM_AXES),
        P(BEAM_AXES, "tensor"),
        P(BEAM_AXES, "tensor"),
        P(BEAM_AXES, "tensor"),
        P(BEAM_AXES, "tensor", None, None),
        P(BEAM_AXES, "tensor", None, None),
        P("tensor", BEAM_AXES),
    )
    out_specs = P("tensor", BEAM_AXES)
    return jax.shard_map(body, mesh=fine, in_specs=in_specs, out_specs=out_specs, check_vma=False)
```

```python
import jax
import jax.numpy as jnp
from jax import lax
from jax.experimental import pallas as pl
from jax.experimental.pallas import tpu as pltpu
from jax.sharding import Mesh
from jax.sharding import PartitionSpec as P

HEAD = 128
GROUPED = 8
SLOTS = 8
BEAMS = 32
POSITIONS = 2048
Q_COLS = GROUPED * HEAD
OUT_COLS = Q_COLS + HEAD
PACKED = 32
BEAM_AXES = ("x", "y", "core")
F32 = jnp.float32
BF16 = jnp.bfloat16
I32 = jnp.int32
MIB = 1024 * 1024
VMEM = pl.BlockSpec(memory_space=pltpu.VMEM)
HBM = pl.BlockSpec(memory_space=pltpu.HBM)


def in_hbm(x):
    return pltpu.with_memory_space_constraint(x, pltpu.HBM)


def beam_index():
    return (lax.axis_index("x") * 4 + lax.axis_index("y")) * 2 + lax.axis_index("core")


def transposed_dot(a, b):
    return lax.dot_general(a, b, (((0,), (0,)), ((), ())), preferred_element_type=F32)


def pack_kernel(
    parent_hbm, len_hbm, q_hbm, key_hbm, value_hbm,
    m0, m1, m2, m3, limit_ref,
    parent_ref, len_ref, q_ref, key_ref, value_ref, head_ref, place_ref, info_ref, sems,
):
    pairs = (
        (parent_hbm, parent_ref),
        (q_hbm, q_ref),
        (key_hbm, key_ref),
        (value_hbm, value_ref),
        (len_hbm, len_ref),
    )
    copies = [pltpu.make_async_copy(a, b, sems.at[n]) for n, (a, b) in enumerate(pairs)]
    for copy in copies:
        copy.start()
    info_ref[...] = jnp.zeros_like(info_ref)
    member = beam_index() % 4
    copies[0].wait()
    partner, order = [], []
    for s in range(SLOTS):
        partner.append((parent_ref[s] // SLOTS) % 4 ^ member)
        earlier = sum([(partner[e] == partner[s]).astype(I32) for e in range(s)], jnp.int32(0))
        order.append(jnp.minimum(earlier, 1))
    for copy in copies[1:4]:
        copy.wait()
    queries = q_ref[...].astype(F32)
    for h in range(GROUPED):
        head_ref[h * SLOTS : (h + 1) * SLOTS, :] = queries[:, h * HEAD : (h + 1) * HEAD]
    fresh_keys = key_ref[...].astype(F32)
    fresh_values = value_ref[...].astype(F32)
    for s in range(SLOTS):
        block = pl.multiple_of(partner[s] * 16 + order[s] * 8, 8)
        place_ref[pl.ds(block, GROUPED), :] = head_ref[pl.ds(s, GROUPED, stride=SLOTS), :]
        row = partner[s] * 16 + order[s]
        cache_row = (parent_ref[s] % SLOTS).astype(F32)
        slot = (member * SLOTS + s).astype(F32)
        info_ref[pl.ds(row, 1), :] = fresh_keys[s : s + 1]
        info_ref[pl.ds(row + 2, 1), :] = fresh_values[s : s + 1]
        info_ref[pl.ds(row + 4, 1), :] = jnp.full((1, HEAD), cache_row, F32)
        info_ref[pl.ds(row + 6, 1), :] = jnp.full((1, HEAD), slot, F32)
    for j, out_ref in enumerate((m0, m1, m2, m3)):
        out_ref[:16, :] = place_ref[j * 16 : j * 16 + 16, :].astype(BF16)
        out_ref[16:, :] = info_ref[j * 16 : j * 16 + 16, :].astype(BF16)
    copies[4].wait()
    rows = lax.broadcasted_iota(I32, (SLOTS, HEAD), 0)
    spread = jnp.zeros((SLOTS, HEAD), I32)
    for r in range(SLOTS):
        spread = jnp.where(rows == r, len_ref[r], spread)
    limit_ref[...] = spread


def load_kernel(after_ref, k_hbm, k_out, sems):
    copies = [
        pltpu.make_async_copy(k_hbm.at[r], k_out.at[r], sems.at[r]) for r in range(SLOTS)
    ]
    for copy in copies:
        copy.start()
    for copy in copies:
        copy.wait()


def attend_kernel(limit_ref, m0, m1, m2, m3, k_ref, v_hbm, out_ref, v_ref, s_ref, o_ref, sems):
    infos = [m[16:, :].astype(F32) for m in (m0, m1, m2, m3)]
    heads = [m[:16, :].astype(F32) for m in (m0, m1, m2, m3)]
    info_ints = [info.astype(I32) for info in infos]
    cache_rows, fetches = [], []
    for i in range(SLOTS):
        row = jnp.clip(info_ints[i // 2][4 + i % 2, 0], 0, SLOTS - 1)
        cache_rows.append(row)
        fetches.append(pltpu.make_async_copy(v_hbm.at[row], v_ref.at[i], sems.at[i]))
        fetches[i].start()
    scale = HEAD ** (-0.5)
    positions = lax.broadcasted_iota(I32, (GROUPED, POSITIONS), 1)
    new_scores = []
    for i in range(SLOTS):
        q = heads[i // 2][i % 2 * 8 : i % 2 * 8 + 8]
        fresh_key = infos[i // 2][i % 2 : i % 2 + 1]
        scores = lax.dot_general(
            q.astype(BF16), k_ref[cache_rows[i]], (((1,), (1,)), ((), ())), preferred_element_type=F32
        ) * scale
        limit = limit_ref[pl.ds(cache_rows[i], 1), :][:, :1]
        s_ref[i] = jnp.where(positions < limit, scores, -1e30)
        new_scores.append(jnp.sum(q * fresh_key, axis=1, keepdims=True) * scale)
    for i in range(SLOTS):
        scores = s_ref[i]
        maximum = jnp.maximum(jnp.max(scores, axis=1, keepdims=True), new_scores[i])
        weights = jnp.exp(scores - maximum)
        new_weight = jnp.exp(new_scores[i] - maximum)
        denominator = jnp.sum(weights, axis=1, keepdims=True) + new_weight
        fetches[i].wait()
        weighted = jnp.dot(weights.astype(BF16), v_ref[i], preferred_element_type=F32)
        fresh_value = infos[i // 2][2 + i % 2 : 3 + i % 2]
        weighted = weighted + new_weight.astype(BF16).astype(F32) * fresh_value
        o_ref[pl.ds(i, GROUPED, stride=SLOTS), :] = weighted / denominator
    ids = jnp.concatenate([info[6:8] for info in infos], axis=0)
    block = jnp.concatenate(
        [o_ref[h * SLOTS : (h + 1) * SLOTS, :] for h in range(GROUPED)] + [ids], axis=1
    )
    pair = jnp.concatenate([block, block], axis=0).astype(BF16)
    for j in range(8):
        out_ref[j * 16 : (j + 1) * 16, :] = pair


def project_kernel(own_ref, other_ref, w_ref, out_ref, place_ref):
    weight = w_ref[...]
    for part, ref in enumerate((own_ref, other_ref)):
        terms = jnp.dot(ref[:, :Q_COLS], weight, preferred_element_type=F32).astype(BF16)
        for g in range(8):
            out_ref[g * 32 + part * 16 : g * 32 + part * 16 + 16, :] = terms[g * 16 : g * 16 + 16]
    first = pl.multiple_of(lax.axis_index("tensor") * 16, 16)
    lanes = lax.broadcasted_iota(I32, (16, HEAD), 1)
    for part, ref in enumerate((own_ref, other_ref)):
        ids = ref[pl.ds(first, 16), Q_COLS:].astype(F32).astype(I32)
        place_ref[part * 16 : part * 16 + 16, :] = (ids == lanes).astype(F32).astype(BF16)


def finish_kernel(terms_ref, place_ref, out_ref):
    total = terms_ref[0:32, :].astype(F32)
    for z in range(1, 8):
        total = total + terms_ref[z * 32 : z * 32 + 32, :].astype(F32)
    out_ref[...] = transposed_dot(place_ref[...], total.astype(BF16))[:BEAMS].astype(BF16)


def pack(parents, lengths, queries, token_keys, token_values):
    message = pltpu.VMEM((PACKED, HEAD), BF16)
    operands = (parents, lengths, queries, token_keys, token_values)
    return pl.pallas_call(
        pack_kernel,
        out_shape=(message,) * 4 + (pltpu.VMEM((SLOTS, HEAD), I32),),
        in_specs=[HBM] * 5,
        out_specs=(VMEM,) * 5,
        scratch_shapes=[
            pltpu.SMEM((SLOTS,), I32),
            pltpu.SMEM((SLOTS,), I32),
            pltpu.VMEM((SLOTS, Q_COLS), BF16),
            pltpu.VMEM((SLOTS, HEAD), BF16),
            pltpu.VMEM((SLOTS, HEAD), BF16),
            pltpu.VMEM((GROUPED * SLOTS, HEAD), F32),
            pltpu.VMEM((GROUPED * SLOTS, HEAD), F32),
            pltpu.VMEM((64, HEAD), F32),
            pltpu.SemaphoreType.DMA((5,)),
        ],
        name="pack",
    )(*[in_hbm(x) for x in operands])


def load(message, key_cache):
    return pl.pallas_call(
        load_kernel,
        out_shape=pltpu.VMEM((SLOTS, POSITIONS, HEAD), BF16),
        in_specs=[VMEM, HBM],
        out_specs=VMEM,
        scratch_shapes=[pltpu.SemaphoreType.DMA((SLOTS,))],
        compiler_params=pltpu.CompilerParams(vmem_limit_bytes=8 * MIB),
        cost_estimate=pl.CostEstimate(flops=0, bytes_accessed=8 * MIB, transcendentals=0),
        name="load",
    )(message, in_hbm(key_cache.reshape(SLOTS, POSITIONS, HEAD)))


def attend(limits, messages, keys, value_cache):
    return pl.pallas_call(
        attend_kernel,
        out_shape=jax.ShapeDtypeStruct((16 * SLOTS, OUT_COLS), BF16),
        in_specs=[VMEM] * 6 + [HBM],
        out_specs=VMEM,
        scratch_shapes=[
            pltpu.VMEM((SLOTS, POSITIONS, HEAD), BF16),
            pltpu.VMEM((SLOTS, GROUPED, POSITIONS), F32),
            pltpu.VMEM((GROUPED * SLOTS, HEAD), F32),
            pltpu.SemaphoreType.DMA((SLOTS,)),
        ],
        compiler_params=pltpu.CompilerParams(vmem_limit_bytes=24 * MIB),
        name="attend",
    )(limits, *messages, keys, in_hbm(value_cache.reshape(SLOTS, POSITIONS, HEAD)))


def body(parents, lengths, queries, token_keys, token_values, key_cache, value_cache, weight):
    *messages, limits = pack(parents, lengths, queries, token_keys, token_values)
    arrived = [
        lax.ppermute(messages[d], BEAM_AXES, [(i, i ^ d) for i in range(32)]) for d in (1, 2, 3)
    ]
    keys = load(messages[0], key_cache)
    heads = attend(limits, [messages[0]] + arrived, keys, value_cache)
    gathered = lax.all_to_all(heads, ("x", "y"), 0, 0, tiled=True)
    other = lax.ppermute(gathered, BEAM_AXES, [(i, i ^ 1) for i in range(32)])
    terms, place = pl.pallas_call(
        project_kernel,
        out_shape=(
            jax.ShapeDtypeStruct((256, 256), BF16),
            jax.ShapeDtypeStruct((BEAMS, HEAD), BF16),
        ),
        in_specs=[VMEM] * 3,
        out_specs=(VMEM, VMEM),
        compiler_params=pltpu.CompilerParams(vmem_limit_bytes=16 * MIB),
        name="project",
    )(gathered, other, weight)
    shares = lax.all_to_all(terms, "tensor", 0, 0, tiled=True)
    return pl.pallas_call(
        finish_kernel,
        out_shape=jax.ShapeDtypeStruct((BEAMS, 256), BF16),
        in_specs=[VMEM] * 2,
        out_specs=VMEM,
        compiler_params=pltpu.CompilerParams(vmem_limit_bytes=16 * MIB),
        name="finish",
    )(shares, place)


def solution(mesh):
    fine = Mesh(mesh.devices.reshape(4, 4, 2, 8), ("x", "y", "core", "tensor"))
    in_specs = (
        P(BEAM_AXES),
        P(BEAM_AXES),
        P(BEAM_AXES, "tensor"),
        P(BEAM_AXES, "tensor"),
        P(BEAM_AXES, "tensor"),
        P(BEAM_AXES, "tensor", None, None),
        P(BEAM_AXES, "tensor", None, None),
        P("tensor", BEAM_AXES),
    )
    out_specs = P("tensor", BEAM_AXES)
    return jax.shard_map(body, mesh=fine, in_specs=in_specs, out_specs=out_specs, check_vma=False)
```

```python
import jax
import jax.numpy as jnp
from jax import lax
from jax.experimental import pallas as pl
from jax.experimental.pallas import tpu as pltpu
from jax.sharding import Mesh
from jax.sharding import PartitionSpec as P

HEAD = 128
GROUPED = 8
SLOTS = 8
BEAMS = 32
POSITIONS = 2048
Q_COLS = GROUPED * HEAD
OUT_COLS = Q_COLS + HEAD
PACKED = 32
BEAM_AXES = ("x", "y", "core")
F32 = jnp.float32
BF16 = jnp.bfloat16
I32 = jnp.int32
MIB = 1024 * 1024
VMEM = pl.BlockSpec(memory_space=pltpu.VMEM)
HBM = pl.BlockSpec(memory_space=pltpu.HBM)


def in_hbm(x):
    return pltpu.with_memory_space_constraint(x, pltpu.HBM)


def beam_index():
    return (lax.axis_index("x") * 4 + lax.axis_index("y")) * 2 + lax.axis_index("core")


def transposed_dot(a, b):
    return lax.dot_general(a, b, (((0,), (0,)), ((), ())), preferred_element_type=F32)


def pack_kernel(
    parent_hbm, len_hbm, q_hbm, key_hbm, value_hbm,
    m0, m1, m2, m3, limit_ref,
    parent_ref, len_ref, q_ref, key_ref, value_ref, head_ref, place_ref, info_ref, sems,
):
    pairs = (
        (parent_hbm, parent_ref),
        (q_hbm, q_ref),
        (key_hbm, key_ref),
        (value_hbm, value_ref),
        (len_hbm, len_ref),
    )
    copies = [pltpu.make_async_copy(a, b, sems.at[n]) for n, (a, b) in enumerate(pairs)]
    for copy in copies:
        copy.start()
    info_ref[...] = jnp.zeros_like(info_ref)
    member = beam_index() % 4
    copies[0].wait()
    partner, order = [], []
    for s in range(SLOTS):
        partner.append((parent_ref[s] // SLOTS) % 4 ^ member)
        earlier = sum([(partner[e] == partner[s]).astype(I32) for e in range(s)], jnp.int32(0))
        order.append(jnp.minimum(earlier, 1))
    for copy in copies[1:4]:
        copy.wait()
    queries = q_ref[...].astype(F32)
    for h in range(GROUPED):
        head_ref[h * SLOTS : (h + 1) * SLOTS, :] = queries[:, h * HEAD : (h + 1) * HEAD]
    fresh_keys = key_ref[...].astype(F32)
    fresh_values = value_ref[...].astype(F32)
    for s in range(SLOTS):
        block = pl.multiple_of(partner[s] * 16 + order[s] * 8, 8)
        place_ref[pl.ds(block, GROUPED), :] = head_ref[pl.ds(s, GROUPED, stride=SLOTS), :]
        row = partner[s] * 16 + order[s]
        cache_row = (parent_ref[s] % SLOTS).astype(F32)
        slot = (member * SLOTS + s).astype(F32)
        info_ref[pl.ds(row, 1), :] = fresh_keys[s : s + 1]
        info_ref[pl.ds(row + 2, 1), :] = fresh_values[s : s + 1]
        info_ref[pl.ds(row + 4, 1), :] = jnp.full((1, HEAD), cache_row, F32)
        info_ref[pl.ds(row + 6, 1), :] = jnp.full((1, HEAD), slot, F32)
    for j, out_ref in enumerate((m0, m1, m2, m3)):
        out_ref[:16, :] = place_ref[j * 16 : j * 16 + 16, :].astype(BF16)
        out_ref[16:, :] = info_ref[j * 16 : j * 16 + 16, :].astype(BF16)
    copies[4].wait()
    rows = lax.broadcasted_iota(I32, (SLOTS, HEAD), 0)
    spread = jnp.zeros((SLOTS, HEAD), I32)
    for r in range(SLOTS):
        spread = jnp.where(rows == r, len_ref[r], spread)
    limit_ref[...] = spread


def attend_kernel(limit_ref, m0, m1, m2, m3, k_ref, v_ref, out_ref, s_ref, o_ref):
    infos = [m[16:, :].astype(F32) for m in (m0, m1, m2, m3)]
    heads = [m[:16, :].astype(F32) for m in (m0, m1, m2, m3)]
    info_ints = [info.astype(I32) for info in infos]
    cache_rows = [
        jnp.clip(info_ints[i // 2][4 + i % 2, 0], 0, SLOTS - 1) for i in range(SLOTS)
    ]
    scale = HEAD ** (-0.5)
    positions = lax.broadcasted_iota(I32, (GROUPED, POSITIONS), 1)
    new_scores = []
    for i in range(SLOTS):
        q = heads[i // 2][i % 2 * 8 : i % 2 * 8 + 8]
        fresh_key = infos[i // 2][i % 2 : i % 2 + 1]
        scores = lax.dot_general(
            q.astype(BF16), k_ref[cache_rows[i]], (((1,), (1,)), ((), ())), preferred_element_type=F32
        ) * scale
        limit = limit_ref[pl.ds(cache_rows[i], 1), :][:, :1]
        s_ref[i] = jnp.where(positions < limit, scores, -1e30)
        new_scores.append(jnp.sum(q * fresh_key, axis=1, keepdims=True) * scale)
    for i in range(SLOTS):
        scores = s_ref[i]
        maximum = jnp.maximum(jnp.max(scores, axis=1, keepdims=True), new_scores[i])
        weights = jnp.exp(scores - maximum)
        new_weight = jnp.exp(new_scores[i] - maximum)
        denominator = jnp.sum(weights, axis=1, keepdims=True) + new_weight
        weighted = jnp.dot(
            weights.astype(BF16), v_ref[cache_rows[i]], preferred_element_type=F32
        )
        fresh_value = infos[i // 2][2 + i % 2 : 3 + i % 2]
        weighted = weighted + new_weight.astype(BF16).astype(F32) * fresh_value
        o_ref[pl.ds(i, GROUPED, stride=SLOTS), :] = weighted / denominator
    ids = jnp.concatenate([info[6:8] for info in infos], axis=0)
    block = jnp.concatenate(
        [o_ref[h * SLOTS : (h + 1) * SLOTS, :] for h in range(GROUPED)] + [ids], axis=1
    )
    pair = jnp.concatenate([block, block], axis=0).astype(BF16)
    for j in range(8):
        out_ref[j * 16 : (j + 1) * 16, :] = pair


def project_kernel(own_ref, other_ref, w_ref, out_ref, place_ref):
    weight = w_ref[...]
    for part, ref in enumerate((own_ref, other_ref)):
        terms = jnp.dot(ref[:, :Q_COLS], weight, preferred_element_type=F32).astype(BF16)
        for g in range(8):
            out_ref[g * 32 + part * 16 : g * 32 + part * 16 + 16, :] = terms[g * 16 : g * 16 + 16]
    first = pl.multiple_of(lax.axis_index("tensor") * 16, 16)
    lanes = lax.broadcasted_iota(I32, (16, HEAD), 1)
    for part, ref in enumerate((own_ref, other_ref)):
        ids = ref[pl.ds(first, 16), Q_COLS:].astype(F32).astype(I32)
        place_ref[part * 16 : part * 16 + 16, :] = (ids == lanes).astype(F32).astype(BF16)


def finish_kernel(terms_ref, place_ref, out_ref):
    total = terms_ref[0:32, :].astype(F32)
    for z in range(1, 8):
        total = total + terms_ref[z * 32 : z * 32 + 32, :].astype(F32)
    out_ref[...] = transposed_dot(place_ref[...], total.astype(BF16))[:BEAMS].astype(BF16)


def pack(parents, lengths, queries, token_keys, token_values):
    message = pltpu.VMEM((PACKED, HEAD), BF16)
    operands = (parents, lengths, queries, token_keys, token_values)
    return pl.pallas_call(
        pack_kernel,
        out_shape=(message,) * 4 + (pltpu.VMEM((SLOTS, HEAD), I32),),
        in_specs=[HBM] * 5,
        out_specs=(VMEM,) * 5,
        scratch_shapes=[
            pltpu.SMEM((SLOTS,), I32),
            pltpu.SMEM((SLOTS,), I32),
            pltpu.VMEM((SLOTS, Q_COLS), BF16),
            pltpu.VMEM((SLOTS, HEAD), BF16),
            pltpu.VMEM((SLOTS, HEAD), BF16),
            pltpu.VMEM((GROUPED * SLOTS, HEAD), F32),
            pltpu.VMEM((GROUPED * SLOTS, HEAD), F32),
            pltpu.VMEM((64, HEAD), F32),
            pltpu.SemaphoreType.DMA((5,)),
        ],
        cost_estimate=pl.CostEstimate(flops=2 * 10**10, bytes_accessed=0, transcendentals=0),
        name="pack",
    )(*[in_hbm(x) for x in operands])


def attend(limits, messages, key_cache, value_cache):
    return pl.pallas_call(
        attend_kernel,
        out_shape=jax.ShapeDtypeStruct((16 * SLOTS, OUT_COLS), BF16),
        in_specs=[VMEM] * 7,
        out_specs=VMEM,
        scratch_shapes=[
            pltpu.VMEM((SLOTS, GROUPED, POSITIONS), F32),
            pltpu.VMEM((GROUPED * SLOTS, HEAD), F32),
        ],
        compiler_params=pltpu.CompilerParams(vmem_limit_bytes=24 * MIB),
        name="attend",
    )(limits, *messages, *[x.reshape(SLOTS, POSITIONS, HEAD) for x in (key_cache, value_cache)])


def body(parents, lengths, queries, token_keys, token_values, key_cache, value_cache, weight):
    *messages, limits = pack(parents, lengths, queries, token_keys, token_values)
    arrived = [
        lax.ppermute(messages[d], BEAM_AXES, [(i, i ^ d) for i in range(32)]) for d in (1, 2, 3)
    ]
    heads = attend(limits, [messages[0]] + arrived, key_cache, value_cache)
    gathered = lax.all_to_all(heads, ("x", "y"), 0, 0, tiled=True)
    other = lax.ppermute(gathered, BEAM_AXES, [(i, i ^ 1) for i in range(32)])
    terms, place = pl.pallas_call(
        project_kernel,
        out_shape=(
            jax.ShapeDtypeStruct((256, 256), BF16),
            jax.ShapeDtypeStruct((BEAMS, HEAD), BF16),
        ),
        in_specs=[VMEM] * 3,
        out_specs=(VMEM, VMEM),
        compiler_params=pltpu.CompilerParams(vmem_limit_bytes=16 * MIB),
        name="project",
    )(gathered, other, weight)
    shares = lax.all_to_all(terms, "tensor", 0, 0, tiled=True)
    return pl.pallas_call(
        finish_kernel,
        out_shape=jax.ShapeDtypeStruct((BEAMS, 256), BF16),
        in_specs=[VMEM] * 2,
        out_specs=VMEM,
        compiler_params=pltpu.CompilerParams(vmem_limit_bytes=16 * MIB),
        name="finish",
    )(shares, place)


def solution(mesh):
    fine = Mesh(mesh.devices.reshape(4, 4, 2, 8), ("x", "y", "core", "tensor"))
    in_specs = (
        P(BEAM_AXES),
        P(BEAM_AXES),
        P(BEAM_AXES, "tensor"),
        P(BEAM_AXES, "tensor"),
        P(BEAM_AXES, "tensor"),
        P(BEAM_AXES, "tensor", None, None),
        P(BEAM_AXES, "tensor", None, None),
        P("tensor", BEAM_AXES),
    )
    out_specs = P("tensor", BEAM_AXES)
    return jax.shard_map(body, mesh=fine, in_specs=in_specs, out_specs=out_specs, check_vma=False)
```

```python
import jax
import jax.numpy as jnp
from jax import lax
from jax.experimental import pallas as pl
from jax.experimental.pallas import tpu as pltpu
from jax.sharding import Mesh
from jax.sharding import PartitionSpec as P

HEAD = 128
GROUPED = 8
SLOTS = 8
BEAMS = 32
POSITIONS = 2048
Q_COLS = GROUPED * HEAD
OUT_COLS = Q_COLS + HEAD
PACKED = 32
BEAM_AXES = ("x", "y", "core")
F32 = jnp.float32
BF16 = jnp.bfloat16
I32 = jnp.int32
MIB = 1024 * 1024
VMEM = pl.BlockSpec(memory_space=pltpu.VMEM)
HBM = pl.BlockSpec(memory_space=pltpu.HBM)


def in_hbm(x):
    return pltpu.with_memory_space_constraint(x, pltpu.HBM)


def beam_index():
    return (lax.axis_index("x") * 4 + lax.axis_index("y")) * 2 + lax.axis_index("core")


def transposed_dot(a, b):
    return lax.dot_general(a, b, (((0,), (0,)), ((), ())), preferred_element_type=F32)


def pack_kernel(
    parent_hbm, len_hbm, q_hbm, key_hbm, value_hbm,
    m0, m1, m2, m3, limit_ref,
    parent_ref, len_ref, q_ref, key_ref, value_ref, head_ref, place_ref, info_ref, sems,
):
    pairs = (
        (parent_hbm, parent_ref),
        (q_hbm, q_ref),
        (key_hbm, key_ref),
        (value_hbm, value_ref),
        (len_hbm, len_ref),
    )
    copies = [pltpu.make_async_copy(a, b, sems.at[n]) for n, (a, b) in enumerate(pairs)]
    for copy in copies:
        copy.start()
    info_ref[...] = jnp.zeros_like(info_ref)
    member = beam_index() & 3
    copies[0].wait()
    partner, order = [], []
    for s in range(SLOTS):
        partner.append((parent_ref[s] >> 3) & 3 ^ member)
        earlier = sum([(partner[e] == partner[s]).astype(I32) for e in range(s)], jnp.int32(0))
        order.append(jnp.minimum(earlier, 1))
    for copy in copies[1:4]:
        copy.wait()
    queries = q_ref[...].astype(F32)
    for h in range(GROUPED):
        head_ref[h * SLOTS : (h + 1) * SLOTS, :] = queries[:, h * HEAD : (h + 1) * HEAD]
    fresh_keys = key_ref[...].astype(F32)
    fresh_values = value_ref[...].astype(F32)
    for s in range(SLOTS):
        block = pl.multiple_of(partner[s] * 16 + order[s] * 8, 8)
        place_ref[pl.ds(block, GROUPED), :] = head_ref[pl.ds(s, GROUPED, stride=SLOTS), :]
        row = partner[s] * 16 + order[s]
        cache_row = (parent_ref[s] & 7).astype(F32)
        slot = (member * SLOTS + s).astype(F32)
        info_ref[pl.ds(row, 1), :] = fresh_keys[s : s + 1]
        info_ref[pl.ds(row + 2, 1), :] = fresh_values[s : s + 1]
        info_ref[pl.ds(row + 4, 1), :] = jnp.full((1, HEAD), cache_row, F32)
        info_ref[pl.ds(row + 6, 1), :] = jnp.full((1, HEAD), slot, F32)
    for j, out_ref in enumerate((m0, m1, m2, m3)):
        out_ref[:16, :] = place_ref[j * 16 : j * 16 + 16, :].astype(BF16)
        out_ref[16:, :] = info_ref[j * 16 : j * 16 + 16, :].astype(BF16)
    copies[4].wait()
    rows = lax.broadcasted_iota(I32, (SLOTS, HEAD), 0)
    spread = jnp.zeros((SLOTS, HEAD), I32)
    for r in range(SLOTS):
        spread = jnp.where(rows == r, len_ref[r], spread)
    limit_ref[...] = spread


def attend_pairs(first, messages, limit_ref, k_ref, v_ref, s_ref, o_ref):
    infos = [m[16:, :].astype(F32) for m in messages]
    heads = [m[:16, :].astype(F32) for m in messages]
    slots = range(2 * len(messages))
    cache_rows = [
        jnp.clip(infos[i // 2].astype(I32)[4 + i % 2, 0], 0, SLOTS - 1) for i in slots
    ]
    scale = HEAD ** (-0.5)
    positions = lax.broadcasted_iota(I32, (GROUPED, POSITIONS), 1)
    new_scores = []
    for i in slots:
        q = heads[i // 2][i % 2 * 8 : i % 2 * 8 + 8]
        fresh_key = infos[i // 2][i % 2 : i % 2 + 1]
        scores = lax.dot_general(
            q.astype(BF16), k_ref[cache_rows[i]], (((1,), (1,)), ((), ())), preferred_element_type=F32
        ) * scale
        limit = limit_ref[pl.ds(cache_rows[i], 1), :][:, :1]
        s_ref[i] = jnp.where(positions < limit, scores, -1e30)
        new_scores.append(jnp.sum(q * fresh_key, axis=1, keepdims=True) * scale)
    for i in slots:
        scores = s_ref[i]
        maximum = jnp.maximum(jnp.max(scores, axis=1, keepdims=True), new_scores[i])
        weights = jnp.exp(scores - maximum)
        new_weight = jnp.exp(new_scores[i] - maximum)
        denominator = jnp.sum(weights, axis=1, keepdims=True) + new_weight
        weighted = jnp.dot(
            weights.astype(BF16), v_ref[cache_rows[i]], preferred_element_type=F32
        )
        fresh_value = infos[i // 2][2 + i % 2 : 3 + i % 2]
        weighted = weighted + new_weight.astype(BF16).astype(F32) * fresh_value
        o_ref[pl.ds(first + i, GROUPED, stride=SLOTS), :] = weighted / denominator


def attend_near_kernel(limit_ref, m0, m1, k_ref, v_ref, o_ref, s_ref):
    o_ref[...] = jnp.zeros_like(o_ref)
    attend_pairs(0, (m0, m1), limit_ref, k_ref, v_ref, s_ref, o_ref)


def attend_next_kernel(limit_ref, before_ref, m2, k_ref, v_ref, o_ref, s_ref):
    o_ref[...] = before_ref[...]
    attend_pairs(4, (m2,), limit_ref, k_ref, v_ref, s_ref, o_ref)


def attend_far_kernel(limit_ref, before_ref, m0, m1, m2, m3, k_ref, v_ref, out_ref, s_ref, o_ref):
    o_ref[...] = before_ref[...]
    attend_pairs(6, (m3,), limit_ref, k_ref, v_ref, s_ref, o_ref)
    ids = jnp.concatenate([m[16:, :].astype(F32)[6:8] for m in (m0, m1, m2, m3)], axis=0)
    block = jnp.concatenate(
        [o_ref[h * SLOTS : (h + 1) * SLOTS, :] for h in range(GROUPED)] + [ids], axis=1
    )
    pair = jnp.concatenate([block, block], axis=0).astype(BF16)
    for j in range(8):
        out_ref[j * 16 : (j + 1) * 16, :] = pair


def project_kernel(own_ref, other_ref, w_ref, out_ref, place_ref):
    weight = w_ref[...]
    for part, ref in enumerate((own_ref, other_ref)):
        terms = jnp.dot(ref[:, :Q_COLS], weight, preferred_element_type=F32).astype(BF16)
        for g in range(8):
            out_ref[g * 32 + part * 16 : g * 32 + part * 16 + 16, :] = terms[g * 16 : g * 16 + 16]
    first = pl.multiple_of(lax.axis_index("tensor") * 16, 16)
    lanes = lax.broadcasted_iota(I32, (16, HEAD), 1)
    for part, ref in enumerate((own_ref, other_ref)):
        ids = ref[pl.ds(first, 16), Q_COLS:].astype(F32).astype(I32)
        place_ref[part * 16 : part * 16 + 16, :] = (ids == lanes).astype(F32).astype(BF16)


def finish_kernel(terms_ref, place_ref, out_ref):
    total = terms_ref[0:32, :].astype(F32)
    for z in range(1, 8):
        total = total + terms_ref[z * 32 : z * 32 + 32, :].astype(F32)
    out_ref[...] = transposed_dot(place_ref[...], total.astype(BF16))[:BEAMS].astype(BF16)


def pack(parents, lengths, queries, token_keys, token_values):
    message = pltpu.VMEM((PACKED, HEAD), BF16)
    operands = (parents, lengths, queries, token_keys, token_values)
    return pl.pallas_call(
        pack_kernel,
        out_shape=(message,) * 4 + (pltpu.VMEM((SLOTS, HEAD), I32),),
        in_specs=[HBM] * 5,
        out_specs=(VMEM,) * 5,
        scratch_shapes=[
            pltpu.SMEM((SLOTS,), I32),
            pltpu.SMEM((SLOTS,), I32),
            pltpu.VMEM((SLOTS, Q_COLS), BF16),
            pltpu.VMEM((SLOTS, HEAD), BF16),
            pltpu.VMEM((SLOTS, HEAD), BF16),
            pltpu.VMEM((GROUPED * SLOTS, HEAD), F32),
            pltpu.VMEM((GROUPED * SLOTS, HEAD), F32),
            pltpu.VMEM((64, HEAD), F32),
            pltpu.SemaphoreType.DMA((5,)),
        ],
        compiler_params=pltpu.CompilerParams(vmem_limit_bytes=4 * MIB),
        cost_estimate=pl.CostEstimate(flops=2 * 10**10, bytes_accessed=0, transcendentals=0),
        name="pack",
    )(*[in_hbm(x) for x in operands])


def attend_early(kernel, slots, name, *operands):
    return pl.pallas_call(
        kernel,
        out_shape=jax.ShapeDtypeStruct((GROUPED * SLOTS, HEAD), F32),
        in_specs=[VMEM] * len(operands),
        out_specs=VMEM,
        scratch_shapes=[pltpu.VMEM((slots, GROUPED, POSITIONS), F32)],
        compiler_params=pltpu.CompilerParams(vmem_limit_bytes=16 * MIB),
        cost_estimate=pl.CostEstimate(flops=2 * 10**9, bytes_accessed=0, transcendentals=0),
        name=name,
    )(*operands)


def attend_far(*operands):
    return pl.pallas_call(
        attend_far_kernel,
        out_shape=jax.ShapeDtypeStruct((16 * SLOTS, OUT_COLS), BF16),
        in_specs=[VMEM] * len(operands),
        out_specs=VMEM,
        scratch_shapes=[
            pltpu.VMEM((2, GROUPED, POSITIONS), F32),
            pltpu.VMEM((GROUPED * SLOTS, HEAD), F32),
        ],
        compiler_params=pltpu.CompilerParams(vmem_limit_bytes=16 * MIB),
        name="attend_far",
    )(*operands)


def body(parents, lengths, queries, token_keys, token_values, key_cache, value_cache, weight):
    *messages, limits = pack(parents, lengths, queries, token_keys, token_values)
    arrived = [
        lax.ppermute(messages[d], BEAM_AXES, [(i, i ^ d) for i in range(32)]) for d in (1, 2, 3)
    ]
    caches = [x.reshape(SLOTS, POSITIONS, HEAD) for x in (key_cache, value_cache)]
    m0, m1, m2, m3 = [messages[0]] + arrived
    part = attend_early(attend_near_kernel, 4, "attend_near", limits, m0, m1, *caches)
    part = attend_early(attend_next_kernel, 2, "attend_next", limits, part, m2, *caches)
    heads = attend_far(limits, part, m0, m1, m2, m3, *caches)
    gathered = lax.all_to_all(heads, ("x", "y"), 0, 0, tiled=True)
    other = lax.ppermute(gathered, BEAM_AXES, [(i, i ^ 1) for i in range(32)])
    terms, place = pl.pallas_call(
        project_kernel,
        out_shape=(
            jax.ShapeDtypeStruct((256, 256), BF16),
            jax.ShapeDtypeStruct((BEAMS, HEAD), BF16),
        ),
        in_specs=[VMEM] * 3,
        out_specs=(VMEM, VMEM),
        compiler_params=pltpu.CompilerParams(vmem_limit_bytes=16 * MIB),
        name="project",
    )(gathered, other, weight)
    shares = lax.all_to_all(terms, "tensor", 0, 0, tiled=True)
    return pl.pallas_call(
        finish_kernel,
        out_shape=jax.ShapeDtypeStruct((BEAMS, 256), BF16),
        in_specs=[VMEM] * 2,
        out_specs=VMEM,
        compiler_params=pltpu.CompilerParams(vmem_limit_bytes=16 * MIB),
        name="finish",
    )(shares, place)


def solution(mesh):
    fine = Mesh(mesh.devices.reshape(4, 4, 2, 8), ("x", "y", "core", "tensor"))
    in_specs = (
        P(BEAM_AXES),
        P(BEAM_AXES),
        P(BEAM_AXES, "tensor"),
        P(BEAM_AXES, "tensor"),
        P(BEAM_AXES, "tensor"),
        P(BEAM_AXES, "tensor", None, None),
        P(BEAM_AXES, "tensor", None, None),
        P("tensor", BEAM_AXES),
    )
    out_specs = P("tensor", BEAM_AXES)
    return jax.shard_map(body, mesh=fine, in_specs=in_specs, out_specs=out_specs, check_vma=False)
```

```python
import jax
import jax.numpy as jnp
from jax import lax
from jax.experimental import pallas as pl
from jax.experimental.pallas import tpu as pltpu
from jax.sharding import PartitionSpec as P

HEAD = 128
GROUPED = 8
SLOTS = 8
BEAMS = 32
POSITIONS = 2048
Q_COLS = GROUPED * HEAD
OUT_COLS = Q_COLS + HEAD
PACKED = 32
BEAM_AXES = "beam"
QUERY_ORDER = (7, 6, 5, 4, 3, 2, 1, 0)
PLANE_ORDER = (4, 5, 6, 7, 0, 1, 2, 3)
CHIP_GROUPS = [[4 * q + 2 * p + c for q in QUERY_ORDER for p in (1, 0)] for c in range(2)]
F32 = jnp.float32
BF16 = jnp.bfloat16
I32 = jnp.int32
MIB = 1024 * 1024
VMEM = pl.BlockSpec(memory_space=pltpu.VMEM)
HBM = pl.BlockSpec(memory_space=pltpu.HBM)


def in_hbm(x):
    return pltpu.with_memory_space_constraint(x, pltpu.HBM)


def beam_index():
    return lax.axis_index("beam")


def transposed_dot(a, b):
    return lax.dot_general(a, b, (((0,), (0,)), ((), ())), preferred_element_type=F32)


def pack_kernel(
    parent_hbm, len_hbm, q_hbm, key_hbm, value_hbm,
    m0, m1, m2, m3, limit_ref,
    parent_ref, len_ref, q_ref, key_ref, value_ref, head_ref, place_ref, info_ref, sems,
):
    pairs = (
        (parent_hbm, parent_ref),
        (q_hbm, q_ref),
        (key_hbm, key_ref),
        (value_hbm, value_ref),
        (len_hbm, len_ref),
    )
    copies = [pltpu.make_async_copy(a, b, sems.at[n]) for n, (a, b) in enumerate(pairs)]
    for copy in copies:
        copy.start()
    info_ref[...] = jnp.zeros_like(info_ref)
    member = beam_index() & 3
    for copy in copies[1:4]:
        copy.wait()
    queries = q_ref[...].astype(F32)
    for h in range(GROUPED):
        head_ref[h * SLOTS : (h + 1) * SLOTS, :] = queries[:, h * HEAD : (h + 1) * HEAD]
    fresh_keys = key_ref[...].astype(F32)
    fresh_values = value_ref[...].astype(F32)
    copies[0].wait()
    copies[4].wait()
    partner, order = [], []
    for s in range(SLOTS):
        partner.append((parent_ref[s] >> 3) & 3 ^ member)
        earlier = jnp.int32(0)
        for e in range(s):
            earlier = jnp.where(partner[e] == partner[s], 1, earlier)
        order.append(earlier)
    rows = lax.broadcasted_iota(I32, (SLOTS, HEAD), 0)
    spread = jnp.zeros((SLOTS, HEAD), I32)
    for s in range(SLOTS):
        block = pl.multiple_of(partner[s] * 16 + order[s] * 8, 8)
        place_ref[pl.ds(block, GROUPED), :] = head_ref[pl.ds(s, GROUPED, stride=SLOTS), :]
        row = partner[s] * 16 + order[s]
        cache_row = (parent_ref[s] & 7).astype(F32)
        slot = (member * SLOTS + s).astype(F32)
        info_ref[pl.ds(row, 1), :] = fresh_keys[s : s + 1]
        info_ref[pl.ds(row + 2, 1), :] = fresh_values[s : s + 1]
        info_ref[pl.ds(row + 4, 1), :] = jnp.full((1, HEAD), cache_row, F32)
        info_ref[pl.ds(row + 6, 1), :] = jnp.full((1, HEAD), slot, F32)
        spread = jnp.where(rows == s, len_ref[s], spread)
    limit_ref[...] = spread
    for j, out_ref in enumerate((m0, m1, m2, m3)):
        out_ref[:16, :] = place_ref[j * 16 : j * 16 + 16, :].astype(BF16)
        out_ref[16:, :] = info_ref[j * 16 : j * 16 + 16, :].astype(BF16)


def attend_pairs(first, messages, limit_ref, k_ref, v_ref, s_ref, o_ref):
    infos = [m[16:, :].astype(F32) for m in messages]
    heads = [m[:16, :].astype(F32) for m in messages]
    slots = range(2 * len(messages))
    cache_rows = [
        jnp.clip(infos[i // 2].astype(I32)[4 + i % 2, 0], 0, SLOTS - 1) for i in slots
    ]
    scale = HEAD ** (-0.5)
    positions = lax.broadcasted_iota(I32, (GROUPED, POSITIONS), 1)
    new_scores = []
    for i in slots:
        q = heads[i // 2][i % 2 * 8 : i % 2 * 8 + 8]
        fresh_key = infos[i // 2][i % 2 : i % 2 + 1]
        scores = lax.dot_general(
            q.astype(BF16), k_ref[cache_rows[i]], (((1,), (1,)), ((), ())), preferred_element_type=F32
        ) * scale
        limit = limit_ref[pl.ds(cache_rows[i], 1), :][:, :1]
        s_ref[i] = jnp.where(positions < limit, scores, -1e30)
        new_scores.append(jnp.sum(q * fresh_key, axis=1, keepdims=True) * scale)
    for i in slots:
        scores = s_ref[i]
        maximum = jnp.maximum(jnp.max(scores, axis=1, keepdims=True), new_scores[i])
        weights = jnp.exp(scores - maximum)
        new_weight = jnp.exp(new_scores[i] - maximum)
        denominator = jnp.sum(weights, axis=1, keepdims=True) + new_weight
        weighted = jnp.dot(
            weights.astype(BF16), v_ref[cache_rows[i]], preferred_element_type=F32
        )
        fresh_value = infos[i // 2][2 + i % 2 : 3 + i % 2]
        weighted = weighted + new_weight.astype(BF16).astype(F32) * fresh_value
        o_ref[pl.ds(first + i, GROUPED, stride=SLOTS), :] = weighted / denominator


def attend_near_kernel(limit_ref, m0, m1, k_ref, v_ref, o_ref, s_ref):
    o_ref[...] = jnp.zeros_like(o_ref)
    attend_pairs(0, (m0, m1), limit_ref, k_ref, v_ref, s_ref, o_ref)


def attend_next_kernel(limit_ref, before_ref, m2, k_ref, v_ref, o_ref, s_ref):
    o_ref[...] = before_ref[...]
    attend_pairs(4, (m2,), limit_ref, k_ref, v_ref, s_ref, o_ref)


def attend_far_kernel(limit_ref, before_ref, m0, m1, m2, m3, k_ref, v_ref, out_ref, s_ref, o_ref):
    o_ref[...] = before_ref[...]
    attend_pairs(6, (m3,), limit_ref, k_ref, v_ref, s_ref, o_ref)
    ids = jnp.concatenate([m[16:, :].astype(F32)[6:8] for m in (m0, m1, m2, m3)], axis=0)
    block = jnp.concatenate(
        [o_ref[h * SLOTS : (h + 1) * SLOTS, :] for h in range(GROUPED)] + [ids], axis=1
    )
    pair = jnp.concatenate([block, block], axis=0).astype(BF16)
    for j in range(8):
        out_ref[j * 16 : (j + 1) * 16, :] = pair


def project_half(part, rows_ref, w_ref, out_ref):
    terms = jnp.dot(rows_ref[:, :Q_COLS], w_ref[...], preferred_element_type=F32).astype(BF16)
    for q in range(8):
        source = QUERY_ORDER.index(q) * 16
        target = PLANE_ORDER.index(q) * 32 + part * 16
        out_ref[target : target + 16, :] = terms[source : source + 16]


def place_half(rows_ref):
    query = lax.axis_index("tensor")
    place = jnp.int32(0)
    for q in range(8):
        place = jnp.where(query == q, QUERY_ORDER.index(q), place)
    first = pl.multiple_of(place * 16, 16)
    lanes = lax.broadcasted_iota(I32, (16, HEAD), 1)
    ids = rows_ref[pl.ds(first, 16), Q_COLS:].astype(F32).astype(I32)
    return (ids == lanes).astype(F32).astype(BF16)


def project_own_kernel(rows_ref, w_ref, out_ref, place_ref):
    project_half(0, rows_ref, w_ref, out_ref)
    place_ref[:16, :] = place_half(rows_ref)
    place_ref[16:, :] = jnp.zeros((16, HEAD), BF16)


def project_other_kernel(rows_ref, w_ref, own_ref, own_place_ref, out_ref, place_ref):
    project_half(1, rows_ref, w_ref, out_ref)
    place_ref[16:, :] = place_half(rows_ref)


def finish_kernel(terms_ref, place_ref, out_ref):
    total = terms_ref[0:32, :].astype(F32)
    for z in range(1, 8):
        total = total + terms_ref[z * 32 : z * 32 + 32, :].astype(F32)
    out_ref[...] = transposed_dot(place_ref[...], total.astype(BF16))[:BEAMS].astype(BF16)


def pack(parents, lengths, queries, token_keys, token_values):
    message = pltpu.VMEM((PACKED, HEAD), BF16)
    operands = (parents, lengths, queries, token_keys, token_values)
    return pl.pallas_call(
        pack_kernel,
        out_shape=(message,) * 4 + (pltpu.VMEM((SLOTS, HEAD), I32),),
        in_specs=[HBM] * 5,
        out_specs=(VMEM,) * 5,
        scratch_shapes=[
            pltpu.SMEM((SLOTS,), I32),
            pltpu.SMEM((SLOTS,), I32),
            pltpu.VMEM((SLOTS, Q_COLS), BF16),
            pltpu.VMEM((SLOTS, HEAD), BF16),
            pltpu.VMEM((SLOTS, HEAD), BF16),
            pltpu.VMEM((GROUPED * SLOTS, HEAD), F32),
            pltpu.VMEM((GROUPED * SLOTS, HEAD), F32),
            pltpu.VMEM((64, HEAD), F32),
            pltpu.SemaphoreType.DMA((5,)),
        ],
        compiler_params=pltpu.CompilerParams(vmem_limit_bytes=4 * MIB),
        cost_estimate=pl.CostEstimate(flops=2 * 10**10, bytes_accessed=0, transcendentals=0),
        name="pack",
    )(*[in_hbm(x) for x in operands])


def attend_early(kernel, slots, name, *operands):
    return pl.pallas_call(
        kernel,
        out_shape=jax.ShapeDtypeStruct((GROUPED * SLOTS, HEAD), F32),
        in_specs=[VMEM] * len(operands),
        out_specs=VMEM,
        scratch_shapes=[pltpu.VMEM((slots, GROUPED, POSITIONS), F32)],
        compiler_params=pltpu.CompilerParams(vmem_limit_bytes=16 * MIB),
        cost_estimate=pl.CostEstimate(flops=2 * 10**9, bytes_accessed=0, transcendentals=0),
        name=name,
    )(*operands)


def attend_far(*operands):
    return pl.pallas_call(
        attend_far_kernel,
        out_shape=jax.ShapeDtypeStruct((16 * SLOTS, OUT_COLS), BF16),
        in_specs=[VMEM] * len(operands),
        out_specs=VMEM,
        scratch_shapes=[
            pltpu.VMEM((2, GROUPED, POSITIONS), F32),
            pltpu.VMEM((GROUPED * SLOTS, HEAD), F32),
        ],
        compiler_params=pltpu.CompilerParams(vmem_limit_bytes=16 * MIB),
        name="attend_far",
    )(*operands)


def body(parents, lengths, queries, token_keys, token_values, key_cache, value_cache, weight):
    *messages, limits = pack(parents, lengths, queries, token_keys, token_values)
    arrived = [
        lax.ppermute(messages[d], BEAM_AXES, [(i, i ^ d) for i in range(32)]) for d in (1, 2, 3)
    ]
    caches = [x.reshape(SLOTS, POSITIONS, HEAD) for x in (key_cache, value_cache)]
    m0, m1, m2, m3 = [messages[0]] + arrived
    part = attend_early(attend_near_kernel, 4, "attend_near", limits, m0, m1, *caches)
    part = attend_early(attend_next_kernel, 2, "attend_next", limits, part, m2, *caches)
    heads = attend_far(limits, part, m0, m1, m2, m3, *caches)
    gathered = lax.all_to_all(heads, "beam", 0, 0, axis_index_groups=CHIP_GROUPS, tiled=True)
    other = lax.ppermute(gathered, BEAM_AXES, [(i, i ^ 1) for i in range(32)])
    shapes = (pltpu.VMEM((256, 256), BF16), pltpu.VMEM((BEAMS, HEAD), BF16))
    params = pltpu.CompilerParams(vmem_limit_bytes=16 * MIB)
    own = pl.pallas_call(
        project_own_kernel,
        out_shape=shapes,
        in_specs=[VMEM] * 2,
        out_specs=(VMEM, VMEM),
        compiler_params=params,
        cost_estimate=pl.CostEstimate(flops=2 * 10**9, bytes_accessed=0, transcendentals=0),
        name="project_own",
    )(gathered, weight)
    terms, place = pl.pallas_call(
        project_other_kernel,
        out_shape=shapes,
        in_specs=[VMEM] * 4,
        out_specs=(VMEM, VMEM),
        input_output_aliases={2: 0, 3: 1},
        compiler_params=params,
        name="project_other",
    )(other, weight, *own)
    shares = lax.all_to_all(
        terms, "tensor", 0, 0, axis_index_groups=[list(PLANE_ORDER)], tiled=True
    )
    return pl.pallas_call(
        finish_kernel,
        out_shape=jax.ShapeDtypeStruct((BEAMS, 256), BF16),
        in_specs=[VMEM] * 2,
        out_specs=VMEM,
        compiler_params=pltpu.CompilerParams(vmem_limit_bytes=16 * MIB),
        name="finish",
    )(shares, place)


def solution(mesh):
    in_specs = (
        P(BEAM_AXES),
        P(BEAM_AXES),
        P(BEAM_AXES, "tensor"),
        P(BEAM_AXES, "tensor"),
        P(BEAM_AXES, "tensor"),
        P(BEAM_AXES, "tensor", None, None),
        P(BEAM_AXES, "tensor", None, None),
        P("tensor", BEAM_AXES),
    )
    out_specs = P("tensor", BEAM_AXES)
    return jax.shard_map(body, mesh=mesh, in_specs=in_specs, out_specs=out_specs, check_vma=False)
```

```python
import jax
import jax.numpy as jnp
from jax import lax
from jax.experimental import pallas as pl
from jax.experimental.pallas import tpu as pltpu
from jax.sharding import PartitionSpec as P

HEAD = 128
GROUPED = 8
SLOTS = 8
BEAMS = 32
POSITIONS = 2048
Q_COLS = GROUPED * HEAD
OUT_COLS = Q_COLS + HEAD
PACKED = 32
BEAM_AXES = "beam"
QUERY_ORDER = (5, 7, 6, 4, 3, 2, 0, 1)
LINE_ORDER = ((4, 0), (4, 1), (5, 0), (5, 1), (6, 0), (0, 1), (6, 1), (7, 0), (7, 1), (1, 1), (0, 0), (1, 0), (3, 0), (2, 0), (2, 1), (3, 1))
LINE_GROUPS = [[(2 * k + c) * 8 + z for z, c in LINE_ORDER] for k in range(16)]
CHIP_GROUPS = [[4 * q + 2 * p + c for q in QUERY_ORDER for p in (1, 0)] for c in range(2)]
F32 = jnp.float32
BF16 = jnp.bfloat16
I32 = jnp.int32
MIB = 1024 * 1024
VMEM = pl.BlockSpec(memory_space=pltpu.VMEM)
HBM = pl.BlockSpec(memory_space=pltpu.HBM)


def in_hbm(x):
    return pltpu.with_memory_space_constraint(x, pltpu.HBM)


def beam_index():
    return lax.axis_index("beam")


def transposed_dot(a, b):
    return lax.dot_general(a, b, (((0,), (0,)), ((), ())), preferred_element_type=F32)


def pack_kernel(
    parent_hbm, len_hbm, q_hbm, key_hbm, value_hbm,
    m0, m1, m2, m3, limit_ref,
    parent_ref, len_ref, q_ref, key_ref, value_ref, head_ref, place_ref, info_ref, sems,
):
    pairs = (
        (parent_hbm, parent_ref),
        (q_hbm, q_ref),
        (key_hbm, key_ref),
        (value_hbm, value_ref),
        (len_hbm, len_ref),
    )
    copies = [pltpu.make_async_copy(a, b, sems.at[n]) for n, (a, b) in enumerate(pairs)]
    for copy in copies:
        copy.start()
    info_ref[...] = jnp.zeros_like(info_ref)
    member = beam_index() & 3
    for copy in copies[1:4]:
        copy.wait()
    queries = q_ref[...].astype(F32)
    for h in range(GROUPED):
        head_ref[h * SLOTS : (h + 1) * SLOTS, :] = queries[:, h * HEAD : (h + 1) * HEAD]
    fresh_keys = key_ref[...].astype(F32)
    fresh_values = value_ref[...].astype(F32)
    copies[0].wait()
    copies[4].wait()
    partner, order = [], []
    for s in range(SLOTS):
        partner.append((parent_ref[s] >> 3) & 3 ^ member)
        earlier = jnp.int32(0)
        for e in range(s):
            earlier = jnp.where(partner[e] == partner[s], 1, earlier)
        order.append(earlier)
    rows = lax.broadcasted_iota(I32, (SLOTS, HEAD), 0)
    spread = jnp.zeros((SLOTS, HEAD), I32)
    for s in range(SLOTS):
        block = pl.multiple_of(partner[s] * 16 + order[s] * 8, 8)
        place_ref[pl.ds(block, GROUPED), :] = head_ref[pl.ds(s, GROUPED, stride=SLOTS), :]
        row = partner[s] * 16 + order[s]
        cache_row = (parent_ref[s] & 7).astype(F32)
        slot = (member * SLOTS + s).astype(F32)
        info_ref[pl.ds(row, 1), :] = fresh_keys[s : s + 1]
        info_ref[pl.ds(row + 2, 1), :] = fresh_values[s : s + 1]
        info_ref[pl.ds(row + 4, 1), :] = jnp.full((1, HEAD), cache_row, F32)
        info_ref[pl.ds(row + 6, 1), :] = jnp.full((1, HEAD), slot, F32)
        beside = (partner[s] ^ 1) * 16 + order[s]
        info_ref[pl.ds(beside + 8, 1), :] = jnp.full((1, HEAD), slot, F32)
        spread = jnp.where(rows == s, len_ref[s], spread)
    limit_ref[...] = spread
    for j, out_ref in enumerate((m0, m1, m2, m3)):
        out_ref[:16, :] = place_ref[j * 16 : j * 16 + 16, :].astype(BF16)
        out_ref[16:, :] = info_ref[j * 16 : j * 16 + 16, :].astype(BF16)


def attend_pairs(first, messages, limit_ref, k_ref, v_ref, s_ref, o_ref):
    infos = [m[16:, :].astype(F32) for m in messages]
    heads = [m[:16, :].astype(F32) for m in messages]
    slots = range(2 * len(messages))
    cache_rows = [
        jnp.clip(infos[i // 2].astype(I32)[4 + i % 2, 0], 0, SLOTS - 1) for i in slots
    ]
    scale = HEAD ** (-0.5)
    positions = lax.broadcasted_iota(I32, (GROUPED, POSITIONS), 1)
    new_scores = []
    for i in slots:
        q = heads[i // 2][i % 2 * 8 : i % 2 * 8 + 8]
        fresh_key = infos[i // 2][i % 2 : i % 2 + 1]
        scores = lax.dot_general(
            q.astype(BF16), k_ref[cache_rows[i]], (((1,), (1,)), ((), ())), preferred_element_type=F32
        ) * scale
        limit = limit_ref[pl.ds(cache_rows[i], 1), :][:, :1]
        s_ref[i] = jnp.where(positions < limit, scores, -1e30)
        new_scores.append(jnp.sum(q * fresh_key, axis=1, keepdims=True) * scale)
    for i in slots:
        scores = s_ref[i]
        maximum = jnp.maximum(jnp.max(scores, axis=1, keepdims=True), new_scores[i])
        weights = jnp.exp(scores - maximum)
        new_weight = jnp.exp(new_scores[i] - maximum)
        denominator = jnp.sum(weights, axis=1, keepdims=True) + new_weight
        weighted = jnp.dot(
            weights.astype(BF16), v_ref[cache_rows[i]], preferred_element_type=F32
        )
        fresh_value = infos[i // 2][2 + i % 2 : 3 + i % 2]
        weighted = weighted + new_weight.astype(BF16).astype(F32) * fresh_value
        o_ref[pl.ds(first + i, GROUPED, stride=SLOTS), :] = weighted / denominator


def attend_near_kernel(limit_ref, m0, m1, k_ref, v_ref, o_ref, s_ref):
    o_ref[...] = jnp.zeros_like(o_ref)
    attend_pairs(0, (m0, m1), limit_ref, k_ref, v_ref, s_ref, o_ref)


def attend_next_kernel(limit_ref, before_ref, m2, k_ref, v_ref, o_ref, s_ref):
    o_ref[...] = before_ref[...]
    attend_pairs(4, (m2,), limit_ref, k_ref, v_ref, s_ref, o_ref)


def attend_far_kernel(limit_ref, before_ref, m0, m1, m2, m3, k_ref, v_ref, out_ref, s_ref, o_ref):
    o_ref[...] = before_ref[...]
    attend_pairs(6, (m3,), limit_ref, k_ref, v_ref, s_ref, o_ref)
    infos = [m[16:, :].astype(F32) for m in (m0, m1, m2, m3)]
    own_ids = jnp.concatenate([info[6:8] for info in infos], axis=0)
    core_ids = jnp.concatenate([infos[d ^ 1][8:10] for d in range(4)], axis=0)
    lanes = lax.broadcasted_iota(I32, (SLOTS, HEAD), 1)
    ids = jnp.where(lanes < HEAD // 2, own_ids, core_ids)
    block = jnp.concatenate(
        [o_ref[h * SLOTS : (h + 1) * SLOTS, :] for h in range(GROUPED)] + [ids], axis=1
    )
    pair = jnp.concatenate([block, block], axis=0).astype(BF16)
    for j in range(8):
        out_ref[j * 16 : (j + 1) * 16, :] = pair


def project_kernel(rows_ref, w_ref, w_core_ref, out_ref, place_ref):
    core = beam_index() & 1
    rows = rows_ref[:, :Q_COLS]
    sides = (core, 1 - core)
    for side, ref in zip(sides, (w_ref, w_core_ref)):
        terms = jnp.dot(rows, ref[...], preferred_element_type=F32).astype(BF16)
        for q in range(8):
            source = QUERY_ORDER.index(q) * 16
            at = jnp.where(side == 0, LINE_ORDER.index((q, 0)), LINE_ORDER.index((q, 1)))
            out_ref[pl.ds(pl.multiple_of(at * 16, 16), 16), :] = terms[source : source + 16]
    query = lax.axis_index("tensor")
    place = jnp.int32(0)
    for q in range(8):
        place = jnp.where(query == q, QUERY_ORDER.index(q), place)
    first = pl.multiple_of(place * 16, 16)
    lanes = lax.broadcasted_iota(I32, (16, HEAD), 1)
    ids = rows_ref[pl.ds(first, 16), Q_COLS:].astype(F32).astype(I32)
    for side, lane in zip(sides, (0, HEAD // 2)):
        place = (ids[:, lane : lane + 1] == lanes).astype(F32).astype(BF16)
        place_ref[pl.ds(pl.multiple_of(side * 16, 16), 16), :] = place


def finish_kernel(terms_ref, place_ref, out_ref):
    halves = []
    for core in range(2):
        total = jnp.zeros((16, 256), F32)
        for at, (_, source_core) in enumerate(LINE_ORDER):
            if source_core == core:
                total = total + terms_ref[at * 16 : at * 16 + 16, :].astype(F32)
        halves.append(total.astype(BF16))
    rows = jnp.concatenate(halves, axis=0)
    out_ref[...] = transposed_dot(place_ref[...], rows)[:BEAMS].astype(BF16)


def pack(parents, lengths, queries, token_keys, token_values):
    message = pltpu.VMEM((PACKED, HEAD), BF16)
    operands = (parents, lengths, queries, token_keys, token_values)
    return pl.pallas_call(
        pack_kernel,
        out_shape=(message,) * 4 + (pltpu.VMEM((SLOTS, HEAD), I32),),
        in_specs=[HBM] * 5,
        out_specs=(VMEM,) * 5,
        scratch_shapes=[
            pltpu.SMEM((SLOTS,), I32),
            pltpu.SMEM((SLOTS,), I32),
            pltpu.VMEM((SLOTS, Q_COLS), BF16),
            pltpu.VMEM((SLOTS, HEAD), BF16),
            pltpu.VMEM((SLOTS, HEAD), BF16),
            pltpu.VMEM((GROUPED * SLOTS, HEAD), F32),
            pltpu.VMEM((GROUPED * SLOTS, HEAD), F32),
            pltpu.VMEM((64, HEAD), F32),
            pltpu.SemaphoreType.DMA((5,)),
        ],
        compiler_params=pltpu.CompilerParams(vmem_limit_bytes=4 * MIB),
        cost_estimate=pl.CostEstimate(flops=2 * 10**10, bytes_accessed=0, transcendentals=0),
        name="pack",
    )(*[in_hbm(x) for x in operands])


def attend_early(kernel, slots, name, *operands):
    return pl.pallas_call(
        kernel,
        out_shape=jax.ShapeDtypeStruct((GROUPED * SLOTS, HEAD), F32),
        in_specs=[VMEM] * len(operands),
        out_specs=VMEM,
        scratch_shapes=[pltpu.VMEM((slots, GROUPED, POSITIONS), F32)],
        compiler_params=pltpu.CompilerParams(vmem_limit_bytes=16 * MIB),
        cost_estimate=pl.CostEstimate(flops=2 * 10**9, bytes_accessed=0, transcendentals=0),
        name=name,
    )(*operands)


def attend_far(*operands):
    return pl.pallas_call(
        attend_far_kernel,
        out_shape=jax.ShapeDtypeStruct((16 * SLOTS, OUT_COLS), BF16),
        in_specs=[VMEM] * len(operands),
        out_specs=VMEM,
        scratch_shapes=[
            pltpu.VMEM((2, GROUPED, POSITIONS), F32),
            pltpu.VMEM((GROUPED * SLOTS, HEAD), F32),
        ],
        compiler_params=pltpu.CompilerParams(vmem_limit_bytes=16 * MIB),
        name="attend_far",
    )(*operands)


def body(parents, lengths, queries, token_keys, token_values, key_cache, value_cache, weight):
    *messages, limits = pack(parents, lengths, queries, token_keys, token_values)
    arrived = [
        lax.ppermute(messages[d], BEAM_AXES, [(i, i ^ d) for i in range(32)]) for d in (1, 2, 3)
    ]
    caches = [x.reshape(SLOTS, POSITIONS, HEAD) for x in (key_cache, value_cache)]
    m0, m1, m2, m3 = [messages[0]] + arrived
    late_weight, m1 = lax.optimization_barrier((weight, m1))
    core_weight = lax.ppermute(late_weight, BEAM_AXES, [(i, i ^ 1) for i in range(32)])
    part = attend_early(attend_near_kernel, 4, "attend_near", limits, m0, m1, *caches)
    part = attend_early(attend_next_kernel, 2, "attend_next", limits, part, m2, *caches)
    heads = attend_far(limits, part, m0, m1, m2, m3, *caches)
    gathered = lax.all_to_all(heads, "beam", 0, 0, axis_index_groups=CHIP_GROUPS, tiled=True)
    terms, place = pl.pallas_call(
        project_kernel,
        out_shape=(pltpu.VMEM((256, 256), BF16), pltpu.VMEM((BEAMS, HEAD), BF16)),
        in_specs=[VMEM] * 3,
        out_specs=(VMEM, VMEM),
        compiler_params=pltpu.CompilerParams(vmem_limit_bytes=16 * MIB),
        name="project",
    )(gathered, weight, core_weight)
    shares = lax.all_to_all(
        terms, ("beam", "tensor"), 0, 0, axis_index_groups=LINE_GROUPS, tiled=True
    )
    return pl.pallas_call(
        finish_kernel,
        out_shape=jax.ShapeDtypeStruct((BEAMS, 256), BF16),
        in_specs=[VMEM] * 2,
        out_specs=VMEM,
        compiler_params=pltpu.CompilerParams(vmem_limit_bytes=16 * MIB),
        name="finish",
    )(shares, place)


def solution(mesh):
    in_specs = (
        P(BEAM_AXES),
        P(BEAM_AXES),
        P(BEAM_AXES, "tensor"),
        P(BEAM_AXES, "tensor"),
        P(BEAM_AXES, "tensor"),
        P(BEAM_AXES, "tensor", None, None),
        P(BEAM_AXES, "tensor", None, None),
        P("tensor", BEAM_AXES),
    )
    out_specs = P("tensor", BEAM_AXES)
    return jax.shard_map(body, mesh=mesh, in_specs=in_specs, out_specs=out_specs, check_vma=False)
```

```python
import jax
import jax.numpy as jnp
from jax import lax
from jax.experimental import pallas as pl
from jax.experimental.pallas import tpu as pltpu
from jax.sharding import PartitionSpec as P

HEAD = 128
GROUPED = 8
SLOTS = 8
BEAMS = 32
POSITIONS = 2048
CHUNK = 1024
Q_COLS = GROUPED * HEAD
OUT_COLS = Q_COLS + HEAD
PACKED = 32
BEAM_AXES = "beam"
QUERY_ORDER = (5, 7, 6, 4, 3, 2, 0, 1)
LINE_ORDER = ((4, 1), (4, 0), (5, 0), (5, 1), (6, 0), (0, 1), (6, 1), (7, 0), (7, 1), (1, 1), (0, 0), (1, 0), (3, 0), (2, 0), (2, 1), (3, 1))
LINE_GROUPS = [[(2 * k + c) * 8 + z for z, c in LINE_ORDER] for k in range(16)]
CHIP_GROUPS = [[4 * q + 2 * p + c for q in QUERY_ORDER for p in (1, 0)] for c in range(2)]
F32 = jnp.float32
BF16 = jnp.bfloat16
I32 = jnp.int32
MIB = 1024 * 1024
VMEM = pl.BlockSpec(memory_space=pltpu.VMEM)
HBM = pl.BlockSpec(memory_space=pltpu.HBM)


def in_hbm(x):
    return pltpu.with_memory_space_constraint(x, pltpu.HBM)


def beam_index():
    return lax.axis_index("beam")


def transposed_dot(a, b):
    return lax.dot_general(a, b, (((0,), (0,)), ((), ())), preferred_element_type=F32)


def pack_kernel(
    parent_hbm, len_hbm, q_hbm, key_hbm, value_hbm,
    m0, m1, m2, m3, limit_ref,
    parent_ref, len_ref, q_ref, key_ref, value_ref, head_ref, place_ref, info_ref, sems,
):
    pairs = (
        (parent_hbm, parent_ref),
        (q_hbm, q_ref),
        (key_hbm, key_ref),
        (value_hbm, value_ref),
        (len_hbm, len_ref),
    )
    copies = [pltpu.make_async_copy(a, b, sems.at[n]) for n, (a, b) in enumerate(pairs)]
    for copy in copies:
        copy.start()
    info_ref[...] = jnp.zeros_like(info_ref)
    member = beam_index() & 3
    for copy in copies[1:4]:
        copy.wait()
    queries = q_ref[...].astype(F32)
    for h in range(GROUPED):
        head_ref[h * SLOTS : (h + 1) * SLOTS, :] = queries[:, h * HEAD : (h + 1) * HEAD]
    fresh_keys = key_ref[...].astype(F32)
    fresh_values = value_ref[...].astype(F32)
    copies[0].wait()
    copies[4].wait()
    partner, order = [], []
    for s in range(SLOTS):
        partner.append((parent_ref[s] >> 3) & 3 ^ member)
        earlier = jnp.int32(0)
        for e in range(s):
            earlier = jnp.where(partner[e] == partner[s], 1, earlier)
        order.append(earlier)
    rows = lax.broadcasted_iota(I32, (SLOTS, HEAD), 0)
    spread = jnp.zeros((SLOTS, HEAD), I32)
    for s in range(SLOTS):
        block = pl.multiple_of(partner[s] * 16 + order[s] * 8, 8)
        place_ref[pl.ds(block, GROUPED), :] = head_ref[pl.ds(s, GROUPED, stride=SLOTS), :]
        row = partner[s] * 16 + order[s]
        cache_row = (parent_ref[s] & 7).astype(F32)
        slot = (member * SLOTS + s).astype(F32)
        info_ref[pl.ds(row, 1), :] = fresh_keys[s : s + 1]
        info_ref[pl.ds(row + 2, 1), :] = fresh_values[s : s + 1]
        info_ref[pl.ds(row + 4, 1), :] = jnp.full((1, HEAD), cache_row, F32)
        info_ref[pl.ds(row + 6, 1), :] = jnp.full((1, HEAD), slot, F32)
        beside = (partner[s] ^ 1) * 16 + order[s]
        info_ref[pl.ds(beside + 8, 1), :] = jnp.full((1, HEAD), slot, F32)
        spread = jnp.where(rows == s, len_ref[s], spread)
    limit_ref[...] = spread
    for j, out_ref in enumerate((m0, m1, m2, m3)):
        out_ref[:16, :] = place_ref[j * 16 : j * 16 + 16, :].astype(BF16)
        out_ref[16:, :] = info_ref[j * 16 : j * 16 + 16, :].astype(BF16)


def attend_pairs(first, messages, limit_ref, k_ref, v_ref, s_ref, o_ref):
    infos = [m[16:, :].astype(F32) for m in messages]
    heads = [m[:16, :].astype(F32) for m in messages]
    slots = range(2 * len(messages))
    cache_rows = [
        jnp.clip(infos[i // 2].astype(I32)[4 + i % 2, 0], 0, SLOTS - 1) for i in slots
    ]
    scale = HEAD ** (-0.5)
    positions = lax.broadcasted_iota(I32, (GROUPED, CHUNK), 1)
    for c in range(POSITIONS // CHUNK):
        for i in slots:
            q = heads[i // 2][i % 2 * 8 : i % 2 * 8 + 8]
            keys = k_ref[cache_rows[i], pl.ds(c * CHUNK, CHUNK), :]
            scores = lax.dot_general(
                q.astype(BF16), keys, (((1,), (1,)), ((), ())), preferred_element_type=F32
            ) * scale
            limit = limit_ref[pl.ds(cache_rows[i], 1), :][:, :1]
            s_ref[i, :, pl.ds(c * CHUNK, CHUNK)] = jnp.where(
                positions + c * CHUNK < limit, scores, -1e30
            )
    for i in slots:
        q = heads[i // 2][i % 2 * 8 : i % 2 * 8 + 8]
        fresh_key = infos[i // 2][i % 2 : i % 2 + 1]
        new_score = jnp.sum(q * fresh_key, axis=1, keepdims=True) * scale
        scores = s_ref[i]
        maximum = jnp.maximum(jnp.max(scores, axis=1, keepdims=True), new_score)
        new_weight = jnp.exp(new_score - maximum)
        denominator = new_weight
        fresh_value = infos[i // 2][2 + i % 2 : 3 + i % 2]
        weighted = new_weight.astype(BF16).astype(F32) * fresh_value
        for c in range(POSITIONS // CHUNK):
            weights = jnp.exp(s_ref[i, :, pl.ds(c * CHUNK, CHUNK)] - maximum)
            denominator = denominator + jnp.sum(weights, axis=1, keepdims=True)
            weighted = weighted + jnp.dot(
                weights.astype(BF16),
                v_ref[cache_rows[i], pl.ds(c * CHUNK, CHUNK), :],
                preferred_element_type=F32,
            )
        o_ref[pl.ds(first + i, GROUPED, stride=SLOTS), :] = weighted / denominator


def attend_near_kernel(limit_ref, m0, m1, k_ref, v_ref, o_ref, s_ref):
    o_ref[...] = jnp.zeros_like(o_ref)
    attend_pairs(0, (m0, m1), limit_ref, k_ref, v_ref, s_ref, o_ref)


def attend_next_kernel(limit_ref, before_ref, m2, k_ref, v_ref, o_ref, s_ref):
    o_ref[...] = before_ref[...]
    attend_pairs(4, (m2,), limit_ref, k_ref, v_ref, s_ref, o_ref)


def attend_far_kernel(limit_ref, before_ref, m0, m1, m2, m3, k_ref, v_ref, out_ref, s_ref, o_ref):
    o_ref[...] = before_ref[...]
    attend_pairs(6, (m3,), limit_ref, k_ref, v_ref, s_ref, o_ref)
    infos = [m[16:, :].astype(F32) for m in (m0, m1, m2, m3)]
    own_ids = jnp.concatenate([info[6:8] for info in infos], axis=0)
    core_ids = jnp.concatenate([infos[d ^ 1][8:10] for d in range(4)], axis=0)
    lanes = lax.broadcasted_iota(I32, (SLOTS, HEAD), 1)
    ids = jnp.where(lanes < HEAD // 2, own_ids, core_ids)
    block = jnp.concatenate(
        [o_ref[h * SLOTS : (h + 1) * SLOTS, :] for h in range(GROUPED)] + [ids], axis=1
    )
    pair = jnp.concatenate([block, block], axis=0).astype(BF16)
    for j in range(8):
        out_ref[j * 16 : (j + 1) * 16, :] = pair


def project_kernel(rows_ref, w_ref, w_core_ref, out_ref, place_ref):
    core = beam_index() & 1
    rows = rows_ref[:, :Q_COLS]
    sides = (core, 1 - core)
    for side, ref in zip(sides, (w_ref, w_core_ref)):
        terms = jnp.dot(rows, ref[...], preferred_element_type=F32).astype(BF16)
        for q in range(8):
            source = QUERY_ORDER.index(q) * 16
            at = jnp.where(side == 0, LINE_ORDER.index((q, 0)), LINE_ORDER.index((q, 1)))
            out_ref[pl.ds(pl.multiple_of(at * 16, 16), 16), :] = terms[source : source + 16]
    query = lax.axis_index("tensor")
    place = jnp.int32(0)
    for q in range(8):
        place = jnp.where(query == q, QUERY_ORDER.index(q), place)
    first = pl.multiple_of(place * 16, 16)
    lanes = lax.broadcasted_iota(I32, (16, HEAD), 1)
    ids = rows_ref[pl.ds(first, 16), Q_COLS:].astype(F32).astype(I32)
    for side, lane in zip(sides, (0, HEAD // 2)):
        place = (ids[:, lane : lane + 1] == lanes).astype(F32).astype(BF16)
        place_ref[pl.ds(pl.multiple_of(side * 16, 16), 16), :] = place


def finish_kernel(terms_ref, place_ref, out_ref):
    halves = []
    for core in range(2):
        total = jnp.zeros((16, 256), F32)
        for at, (_, source_core) in enumerate(LINE_ORDER):
            if source_core == core:
                total = total + terms_ref[at * 16 : at * 16 + 16, :].astype(F32)
        halves.append(total.astype(BF16))
    rows = jnp.concatenate(halves, axis=0)
    out_ref[...] = transposed_dot(place_ref[...], rows)[:BEAMS].astype(BF16)


def pack(parents, lengths, queries, token_keys, token_values):
    message = pltpu.VMEM((PACKED, HEAD), BF16)
    operands = (parents, lengths, queries, token_keys, token_values)
    return pl.pallas_call(
        pack_kernel,
        out_shape=(message,) * 4 + (pltpu.VMEM((SLOTS, HEAD), I32),),
        in_specs=[HBM] * 5,
        out_specs=(VMEM,) * 5,
        scratch_shapes=[
            pltpu.SMEM((SLOTS,), I32),
            pltpu.SMEM((SLOTS,), I32),
            pltpu.VMEM((SLOTS, Q_COLS), BF16),
            pltpu.VMEM((SLOTS, HEAD), BF16),
            pltpu.VMEM((SLOTS, HEAD), BF16),
            pltpu.VMEM((GROUPED * SLOTS, HEAD), F32),
            pltpu.VMEM((GROUPED * SLOTS, HEAD), F32),
            pltpu.VMEM((64, HEAD), F32),
            pltpu.SemaphoreType.DMA((5,)),
        ],
        compiler_params=pltpu.CompilerParams(vmem_limit_bytes=4 * MIB),
        cost_estimate=pl.CostEstimate(flops=2 * 10**10, bytes_accessed=0, transcendentals=0),
        name="pack",
    )(*[in_hbm(x) for x in operands])


def attend_early(kernel, slots, name, *operands):
    return pl.pallas_call(
        kernel,
        out_shape=jax.ShapeDtypeStruct((GROUPED * SLOTS, HEAD), F32),
        in_specs=[VMEM] * len(operands),
        out_specs=VMEM,
        scratch_shapes=[pltpu.VMEM((slots, GROUPED, POSITIONS), F32)],
        compiler_params=pltpu.CompilerParams(vmem_limit_bytes=16 * MIB),
        cost_estimate=pl.CostEstimate(flops=2 * 10**9, bytes_accessed=0, transcendentals=0),
        name=name,
    )(*operands)


def attend_far(*operands):
    return pl.pallas_call(
        attend_far_kernel,
        out_shape=jax.ShapeDtypeStruct((16 * SLOTS, OUT_COLS), BF16),
        in_specs=[VMEM] * len(operands),
        out_specs=VMEM,
        scratch_shapes=[
            pltpu.VMEM((2, GROUPED, POSITIONS), F32),
            pltpu.VMEM((GROUPED * SLOTS, HEAD), F32),
        ],
        compiler_params=pltpu.CompilerParams(vmem_limit_bytes=16 * MIB),
        name="attend_far",
    )(*operands)


def body(parents, lengths, queries, token_keys, token_values, key_cache, value_cache, weight):
    *messages, limits = pack(parents, lengths, queries, token_keys, token_values)
    arrived = [
        lax.ppermute(messages[d], BEAM_AXES, [(i, i ^ d) for i in range(32)]) for d in (1, 2, 3)
    ]
    caches = [x.reshape(SLOTS, POSITIONS, HEAD) for x in (key_cache, value_cache)]
    m0, m1, m2, m3 = [messages[0]] + arrived
    late_weight, m1 = lax.optimization_barrier((weight, m1))
    core_weight = lax.ppermute(late_weight, BEAM_AXES, [(i, i ^ 1) for i in range(32)])
    part = attend_early(attend_near_kernel, 4, "attend_near", limits, m0, m1, *caches)
    part = attend_early(attend_next_kernel, 2, "attend_next", limits, part, m2, *caches)
    heads = attend_far(limits, part, m0, m1, m2, m3, *caches)
    gathered = lax.all_to_all(heads, "beam", 0, 0, axis_index_groups=CHIP_GROUPS, tiled=True)
    terms, place = pl.pallas_call(
        project_kernel,
        out_shape=(pltpu.VMEM((256, 256), BF16), pltpu.VMEM((BEAMS, HEAD), BF16)),
        in_specs=[VMEM] * 3,
        out_specs=(VMEM, VMEM),
        compiler_params=pltpu.CompilerParams(vmem_limit_bytes=16 * MIB),
        name="project",
    )(gathered, weight, core_weight)
    shares = lax.all_to_all(
        terms, ("beam", "tensor"), 0, 0, axis_index_groups=LINE_GROUPS, tiled=True
    )
    return pl.pallas_call(
        finish_kernel,
        out_shape=jax.ShapeDtypeStruct((BEAMS, 256), BF16),
        in_specs=[VMEM] * 2,
        out_specs=VMEM,
        compiler_params=pltpu.CompilerParams(vmem_limit_bytes=16 * MIB),
        name="finish",
    )(shares, place)


def solution(mesh):
    in_specs = (
        P(BEAM_AXES),
        P(BEAM_AXES),
        P(BEAM_AXES, "tensor"),
        P(BEAM_AXES, "tensor"),
        P(BEAM_AXES, "tensor"),
        P(BEAM_AXES, "tensor", None, None),
        P(BEAM_AXES, "tensor", None, None),
        P("tensor", BEAM_AXES),
    )
    out_specs = P("tensor", BEAM_AXES)
    return jax.shard_map(body, mesh=mesh, in_specs=in_specs, out_specs=out_specs, check_vma=False)
```

```python
import jax
import jax.numpy as jnp
from jax import lax
from jax.experimental import pallas as pl
from jax.experimental.pallas import tpu as pltpu
from jax.sharding import PartitionSpec as P

HEAD = 128
GROUPED = 8
SLOTS = 8
BEAMS = 32
POSITIONS = 2048
CHUNK = 1024
Q_COLS = GROUPED * HEAD
OUT_COLS = Q_COLS + HEAD
PACKED = 32
BEAM_AXES = "beam"
QUERY_ORDER = (5, 7, 6, 4, 3, 2, 0, 1)
LINE_ORDER = ((5, 1), (4, 0), (5, 0), (4, 1), (6, 0), (0, 1), (6, 1), (7, 0), (7, 1), (1, 1), (0, 0), (1, 0), (3, 0), (2, 0), (2, 1), (3, 1))
LINE_GROUPS = [[(2 * k + c) * 8 + z for z, c in LINE_ORDER] for k in range(16)]
CHIP_GROUPS = [[4 * q + 2 * p + c for q in QUERY_ORDER for p in (1, 0)] for c in range(2)]
F32 = jnp.float32
BF16 = jnp.bfloat16
I32 = jnp.int32
MIB = 1024 * 1024
VMEM = pl.BlockSpec(memory_space=pltpu.VMEM)
HBM = pl.BlockSpec(memory_space=pltpu.HBM)


def in_hbm(x):
    return pltpu.with_memory_space_constraint(x, pltpu.HBM)


def beam_index():
    return lax.axis_index("beam")


def transposed_dot(a, b):
    return lax.dot_general(a, b, (((0,), (0,)), ((), ())), preferred_element_type=F32)


def pack_kernel(
    parent_hbm, len_hbm, q_hbm, key_hbm, value_hbm,
    m0, m1, m2, m3, limit_ref,
    parent_ref, len_ref, q_ref, key_ref, value_ref, head_ref, place_ref, info_ref, sems,
):
    pairs = (
        (parent_hbm, parent_ref),
        (q_hbm, q_ref),
        (key_hbm, key_ref),
        (value_hbm, value_ref),
        (len_hbm, len_ref),
    )
    copies = [pltpu.make_async_copy(a, b, sems.at[n]) for n, (a, b) in enumerate(pairs)]
    for copy in copies:
        copy.start()
    info_ref[...] = jnp.zeros_like(info_ref)
    member = beam_index() & 3
    for copy in copies[1:4]:
        copy.wait()
    queries = q_ref[...].astype(F32)
    for h in range(GROUPED):
        head_ref[h * SLOTS : (h + 1) * SLOTS, :] = queries[:, h * HEAD : (h + 1) * HEAD]
    fresh_keys = key_ref[...].astype(F32)
    fresh_values = value_ref[...].astype(F32)
    copies[0].wait()
    copies[4].wait()
    partner, order = [], []
    for s in range(SLOTS):
        partner.append((parent_ref[s] >> 3) & 3 ^ member)
        earlier = jnp.int32(0)
        for e in range(s):
            earlier = jnp.where(partner[e] == partner[s], 1, earlier)
        order.append(earlier)
    rows = lax.broadcasted_iota(I32, (SLOTS, HEAD), 0)
    spread = jnp.zeros((SLOTS, HEAD), I32)
    for s in range(SLOTS):
        block = pl.multiple_of(partner[s] * 16 + order[s] * 8, 8)
        place_ref[pl.ds(block, GROUPED), :] = head_ref[pl.ds(s, GROUPED, stride=SLOTS), :]
        row = partner[s] * 16 + order[s]
        cache_row = (parent_ref[s] & 7).astype(F32)
        slot = (member * SLOTS + s).astype(F32)
        info_ref[pl.ds(row, 1), :] = fresh_keys[s : s + 1]
        info_ref[pl.ds(row + 2, 1), :] = fresh_values[s : s + 1]
        info_ref[pl.ds(row + 4, 1), :] = jnp.full((1, HEAD), cache_row, F32)
        info_ref[pl.ds(row + 6, 1), :] = jnp.full((1, HEAD), slot, F32)
        beside = (partner[s] ^ 1) * 16 + order[s]
        info_ref[pl.ds(beside + 8, 1), :] = jnp.full((1, HEAD), slot, F32)
        spread = jnp.where(rows == s, len_ref[s], spread)
    limit_ref[...] = spread
    for j, out_ref in enumerate((m0, m1, m2, m3)):
        out_ref[:16, :] = place_ref[j * 16 : j * 16 + 16, :].astype(BF16)
        out_ref[16:, :] = info_ref[j * 16 : j * 16 + 16, :].astype(BF16)


def attend_pairs(first, messages, limit_ref, k_ref, v_ref, s_ref, o_ref):
    infos = [m[16:, :].astype(F32) for m in messages]
    heads = [m[:16, :].astype(F32) for m in messages]
    slots = range(2 * len(messages))
    cache_rows = [
        jnp.clip(infos[i // 2].astype(I32)[4 + i % 2, 0], 0, SLOTS - 1) for i in slots
    ]
    scale = HEAD ** (-0.5)
    positions = lax.broadcasted_iota(I32, (GROUPED, CHUNK), 1)
    for c in range(POSITIONS // CHUNK):
        for i in slots:
            q = heads[i // 2][i % 2 * 8 : i % 2 * 8 + 8]
            keys = k_ref[cache_rows[i], pl.ds(c * CHUNK, CHUNK), :]
            scores = lax.dot_general(
                q.astype(BF16), keys, (((1,), (1,)), ((), ())), preferred_element_type=F32
            ) * scale
            limit = limit_ref[pl.ds(cache_rows[i], 1), :][:, :1]
            s_ref[i, :, pl.ds(c * CHUNK, CHUNK)] = jnp.where(
                positions + c * CHUNK < limit, scores, -1e30
            )
    for i in slots:
        q = heads[i // 2][i % 2 * 8 : i % 2 * 8 + 8]
        fresh_key = infos[i // 2][i % 2 : i % 2 + 1]
        new_score = jnp.sum(q * fresh_key, axis=1, keepdims=True) * scale
        scores = s_ref[i]
        maximum = jnp.maximum(jnp.max(scores, axis=1, keepdims=True), new_score)
        new_weight = jnp.exp(new_score - maximum)
        denominator = new_weight
        fresh_value = infos[i // 2][2 + i % 2 : 3 + i % 2]
        weighted = new_weight.astype(BF16).astype(F32) * fresh_value
        for c in range(POSITIONS // CHUNK):
            weights = jnp.exp(s_ref[i, :, pl.ds(c * CHUNK, CHUNK)] - maximum)
            denominator = denominator + jnp.sum(weights, axis=1, keepdims=True)
            weighted = weighted + jnp.dot(
                weights.astype(BF16),
                v_ref[cache_rows[i], pl.ds(c * CHUNK, CHUNK), :],
                preferred_element_type=F32,
            )
        o_ref[pl.ds(first + i, GROUPED, stride=SLOTS), :] = weighted / denominator


def attend_near_kernel(limit_ref, m0, m1, k_ref, v_ref, o_ref, s_ref):
    o_ref[...] = jnp.zeros_like(o_ref)
    attend_pairs(0, (m0, m1), limit_ref, k_ref, v_ref, s_ref, o_ref)


def attend_next_kernel(limit_ref, before_ref, m2, k_ref, v_ref, o_ref, s_ref):
    o_ref[...] = before_ref[...]
    attend_pairs(4, (m2,), limit_ref, k_ref, v_ref, s_ref, o_ref)


def attend_far_kernel(limit_ref, before_ref, m0, m1, m2, m3, k_ref, v_ref, out_ref, s_ref, o_ref):
    o_ref[...] = before_ref[...]
    attend_pairs(6, (m3,), limit_ref, k_ref, v_ref, s_ref, o_ref)
    infos = [m[16:, :].astype(F32) for m in (m0, m1, m2, m3)]
    own_ids = jnp.concatenate([info[6:8] for info in infos], axis=0)
    core_ids = jnp.concatenate([infos[d ^ 1][8:10] for d in range(4)], axis=0)
    lanes = lax.broadcasted_iota(I32, (SLOTS, HEAD), 1)
    ids = jnp.where(lanes < HEAD // 2, own_ids, core_ids)
    block = jnp.concatenate(
        [o_ref[h * SLOTS : (h + 1) * SLOTS, :] for h in range(GROUPED)] + [ids], axis=1
    )
    pair = jnp.concatenate([block, block], axis=0).astype(BF16)
    for j in range(8):
        out_ref[j * 16 : (j + 1) * 16, :] = pair


def project_kernel(rows_ref, w_ref, w_core_ref, out_ref, place_ref):
    core = beam_index() & 1
    rows = rows_ref[:, :Q_COLS]
    sides = (core, 1 - core)
    for side, ref in zip(sides, (w_ref, w_core_ref)):
        terms = jnp.dot(rows, ref[...], preferred_element_type=F32).astype(BF16)
        for q in range(8):
            source = QUERY_ORDER.index(q) * 16
            at = jnp.where(side == 0, LINE_ORDER.index((q, 0)), LINE_ORDER.index((q, 1)))
            out_ref[pl.ds(pl.multiple_of(at * 16, 16), 16), :] = terms[source : source + 16]
    query = lax.axis_index("tensor")
    place = jnp.int32(0)
    for q in range(8):
        place = jnp.where(query == q, QUERY_ORDER.index(q), place)
    first = pl.multiple_of(place * 16, 16)
    lanes = lax.broadcasted_iota(I32, (16, HEAD), 1)
    ids = rows_ref[pl.ds(first, 16), Q_COLS:].astype(F32).astype(I32)
    for side, lane in zip(sides, (0, HEAD // 2)):
        place = (ids[:, lane : lane + 1] == lanes).astype(F32).astype(BF16)
        place_ref[pl.ds(pl.multiple_of(side * 16, 16), 16), :] = place


def finish_kernel(terms_ref, place_ref, out_ref):
    halves = []
    for core in range(2):
        total = jnp.zeros((16, 256), F32)
        for at, (_, source_core) in enumerate(LINE_ORDER):
            if source_core == core:
                total = total + terms_ref[at * 16 : at * 16 + 16, :].astype(F32)
        halves.append(total.astype(BF16))
    rows = jnp.concatenate(halves, axis=0)
    out_ref[...] = transposed_dot(place_ref[...], rows)[:BEAMS].astype(BF16)


def pack(parents, lengths, queries, token_keys, token_values):
    message = pltpu.VMEM((PACKED, HEAD), BF16)
    operands = (parents, lengths, queries, token_keys, token_values)
    return pl.pallas_call(
        pack_kernel,
        out_shape=(message,) * 4 + (pltpu.VMEM((SLOTS, HEAD), I32),),
        in_specs=[HBM] * 5,
        out_specs=(VMEM,) * 5,
        scratch_shapes=[
            pltpu.SMEM((SLOTS,), I32),
            pltpu.SMEM((SLOTS,), I32),
            pltpu.VMEM((SLOTS, Q_COLS), BF16),
            pltpu.VMEM((SLOTS, HEAD), BF16),
            pltpu.VMEM((SLOTS, HEAD), BF16),
            pltpu.VMEM((GROUPED * SLOTS, HEAD), F32),
            pltpu.VMEM((GROUPED * SLOTS, HEAD), F32),
            pltpu.VMEM((64, HEAD), F32),
            pltpu.SemaphoreType.DMA((5,)),
        ],
        compiler_params=pltpu.CompilerParams(vmem_limit_bytes=4 * MIB),
        cost_estimate=pl.CostEstimate(flops=2 * 10**10, bytes_accessed=0, transcendentals=0),
        name="pack",
    )(*[in_hbm(x) for x in operands])


def attend_early(kernel, slots, name, *operands):
    return pl.pallas_call(
        kernel,
        out_shape=jax.ShapeDtypeStruct((GROUPED * SLOTS, HEAD), F32),
        in_specs=[VMEM] * len(operands),
        out_specs=VMEM,
        scratch_shapes=[pltpu.VMEM((slots, GROUPED, POSITIONS), F32)],
        compiler_params=pltpu.CompilerParams(vmem_limit_bytes=16 * MIB),
        cost_estimate=pl.CostEstimate(flops=2 * 10**9, bytes_accessed=0, transcendentals=0),
        name=name,
    )(*operands)


def attend_far(*operands):
    return pl.pallas_call(
        attend_far_kernel,
        out_shape=jax.ShapeDtypeStruct((16 * SLOTS, OUT_COLS), BF16),
        in_specs=[VMEM] * len(operands),
        out_specs=VMEM,
        scratch_shapes=[
            pltpu.VMEM((2, GROUPED, POSITIONS), F32),
            pltpu.VMEM((GROUPED * SLOTS, HEAD), F32),
        ],
        compiler_params=pltpu.CompilerParams(vmem_limit_bytes=16 * MIB),
        name="attend_far",
    )(*operands)


def body(parents, lengths, queries, token_keys, token_values, key_cache, value_cache, weight):
    *messages, limits = pack(parents, lengths, queries, token_keys, token_values)
    arrived = [
        lax.ppermute(messages[d], BEAM_AXES, [(i, i ^ d) for i in range(32)]) for d in (1, 2, 3)
    ]
    caches = [x.reshape(SLOTS, POSITIONS, HEAD) for x in (key_cache, value_cache)]
    m0, m1, m2, m3 = [messages[0]] + arrived
    late_weight, m1 = lax.optimization_barrier((weight, m1))
    core_weight = lax.ppermute(late_weight, BEAM_AXES, [(i, i ^ 1) for i in range(32)])
    part = attend_early(attend_near_kernel, 4, "attend_near", limits, m0, m1, *caches)
    part = attend_early(attend_next_kernel, 2, "attend_next", limits, part, m2, *caches)
    heads = attend_far(limits, part, m0, m1, m2, m3, *caches)
    gathered = lax.all_to_all(heads, "beam", 0, 0, axis_index_groups=CHIP_GROUPS, tiled=True)
    terms, place = pl.pallas_call(
        project_kernel,
        out_shape=(pltpu.VMEM((256, 256), BF16), pltpu.VMEM((BEAMS, HEAD), BF16)),
        in_specs=[VMEM] * 3,
        out_specs=(VMEM, VMEM),
        compiler_params=pltpu.CompilerParams(vmem_limit_bytes=16 * MIB),
        name="project",
    )(gathered, weight, core_weight)
    shares = lax.all_to_all(
        terms, ("beam", "tensor"), 0, 0, axis_index_groups=LINE_GROUPS, tiled=True
    )
    return pl.pallas_call(
        finish_kernel,
        out_shape=jax.ShapeDtypeStruct((BEAMS, 256), BF16),
        in_specs=[VMEM] * 2,
        out_specs=VMEM,
        compiler_params=pltpu.CompilerParams(vmem_limit_bytes=16 * MIB),
        name="finish",
    )(shares, place)


def solution(mesh):
    in_specs = (
        P(BEAM_AXES),
        P(BEAM_AXES),
        P(BEAM_AXES, "tensor"),
        P(BEAM_AXES, "tensor"),
        P(BEAM_AXES, "tensor"),
        P(BEAM_AXES, "tensor", None, None),
        P(BEAM_AXES, "tensor", None, None),
        P("tensor", BEAM_AXES),
    )
    out_specs = P("tensor", BEAM_AXES)
    return jax.shard_map(body, mesh=mesh, in_specs=in_specs, out_specs=out_specs, check_vma=False)
```

```python
import jax
import jax.numpy as jnp
from jax import lax
from jax.experimental import pallas as pl
from jax.experimental.pallas import tpu as pltpu
from jax.sharding import PartitionSpec as P

HEAD = 128
GROUPED = 8
SLOTS = 8
BEAMS = 32
POSITIONS = 2048
CHUNK = 1024
Q_COLS = GROUPED * HEAD
OUT_COLS = Q_COLS + HEAD
PACKED = 32
BEAM_AXES = "beam"
QUERY_ORDER = (5, 7, 6, 1, 3, 2, 0, 4)
LINE_ORDER = ((5, 1), (4, 0), (5, 0), (4, 1), (6, 0), (0, 1), (6, 1), (7, 0), (7, 1), (1, 1), (0, 0), (1, 0), (3, 0), (2, 0), (2, 1), (3, 1))
LINE_GROUPS = [[(2 * k + c) * 8 + z for z, c in LINE_ORDER] for k in range(16)]
CHIP_GROUPS = [[4 * q + 2 * p + c for q in QUERY_ORDER for p in (1, 0)] for c in range(2)]
F32 = jnp.float32
BF16 = jnp.bfloat16
I32 = jnp.int32
MIB = 1024 * 1024
VMEM = pl.BlockSpec(memory_space=pltpu.VMEM)
HBM = pl.BlockSpec(memory_space=pltpu.HBM)


def in_hbm(x):
    return pltpu.with_memory_space_constraint(x, pltpu.HBM)


def beam_index():
    return lax.axis_index("beam")


def transposed_dot(a, b):
    return lax.dot_general(a, b, (((0,), (0,)), ((), ())), preferred_element_type=F32)


def pack_kernel(
    parent_hbm, len_hbm, q_hbm, key_hbm, value_hbm,
    m0, m1, m2, m3, limit_ref,
    parent_ref, len_ref, q_ref, key_ref, value_ref, head_ref, place_ref, info_ref, sems,
):
    pairs = (
        (parent_hbm, parent_ref),
        (q_hbm, q_ref),
        (key_hbm, key_ref),
        (value_hbm, value_ref),
        (len_hbm, len_ref),
    )
    copies = [pltpu.make_async_copy(a, b, sems.at[n]) for n, (a, b) in enumerate(pairs)]
    for copy in copies:
        copy.start()
    info_ref[...] = jnp.zeros_like(info_ref)
    member = beam_index() & 3
    for copy in copies[1:4]:
        copy.wait()
    queries = q_ref[...].astype(F32)
    for h in range(GROUPED):
        head_ref[h * SLOTS : (h + 1) * SLOTS, :] = queries[:, h * HEAD : (h + 1) * HEAD]
    fresh_keys = key_ref[...].astype(F32)
    fresh_values = value_ref[...].astype(F32)
    copies[0].wait()
    copies[4].wait()
    partner, order = [], []
    for s in range(SLOTS):
        partner.append((parent_ref[s] >> 3) & 3 ^ member)
        earlier = jnp.int32(0)
        for e in range(s):
            earlier = jnp.where(partner[e] == partner[s], 1, earlier)
        order.append(earlier)
    rows = lax.broadcasted_iota(I32, (SLOTS, HEAD), 0)
    spread = jnp.zeros((SLOTS, HEAD), I32)
    for s in range(SLOTS):
        block = pl.multiple_of(partner[s] * 16 + order[s] * 8, 8)
        place_ref[pl.ds(block, GROUPED), :] = head_ref[pl.ds(s, GROUPED, stride=SLOTS), :]
        row = partner[s] * 16 + order[s]
        cache_row = (parent_ref[s] & 7).astype(F32)
        slot = (member * SLOTS + s).astype(F32)
        info_ref[pl.ds(row, 1), :] = fresh_keys[s : s + 1]
        info_ref[pl.ds(row + 2, 1), :] = fresh_values[s : s + 1]
        info_ref[pl.ds(row + 4, 1), :] = jnp.full((1, HEAD), cache_row, F32)
        info_ref[pl.ds(row + 6, 1), :] = jnp.full((1, HEAD), slot, F32)
        beside = (partner[s] ^ 1) * 16 + order[s]
        info_ref[pl.ds(beside + 8, 1), :] = jnp.full((1, HEAD), slot, F32)
        spread = jnp.where(rows == s, len_ref[s], spread)
    limit_ref[...] = spread
    for j, out_ref in enumerate((m0, m1, m2, m3)):
        out_ref[:16, :] = place_ref[j * 16 : j * 16 + 16, :].astype(BF16)
        out_ref[16:, :] = info_ref[j * 16 : j * 16 + 16, :].astype(BF16)


def attend_pairs(first, messages, limit_ref, k_ref, v_ref, s_ref, o_ref):
    infos = [m[16:, :].astype(F32) for m in messages]
    heads = [m[:16, :].astype(F32) for m in messages]
    slots = range(2 * len(messages))
    cache_rows = [
        jnp.clip(infos[i // 2].astype(I32)[4 + i % 2, 0], 0, SLOTS - 1) for i in slots
    ]
    scale = HEAD ** (-0.5)
    positions = lax.broadcasted_iota(I32, (GROUPED, CHUNK), 1)
    for c in range(POSITIONS // CHUNK):
        for i in slots:
            q = heads[i // 2][i % 2 * 8 : i % 2 * 8 + 8]
            keys = k_ref[cache_rows[i], pl.ds(c * CHUNK, CHUNK), :]
            scores = lax.dot_general(
                q.astype(BF16), keys, (((1,), (1,)), ((), ())), preferred_element_type=F32
            ) * scale
            limit = limit_ref[pl.ds(cache_rows[i], 1), :][:, :1]
            s_ref[i, :, pl.ds(c * CHUNK, CHUNK)] = jnp.where(
                positions + c * CHUNK < limit, scores, -1e30
            )
    for i in slots:
        q = heads[i // 2][i % 2 * 8 : i % 2 * 8 + 8]
        fresh_key = infos[i // 2][i % 2 : i % 2 + 1]
        new_score = jnp.sum(q * fresh_key, axis=1, keepdims=True) * scale
        scores = s_ref[i]
        maximum = jnp.maximum(jnp.max(scores, axis=1, keepdims=True), new_score)
        new_weight = jnp.exp(new_score - maximum)
        denominator = new_weight
        fresh_value = infos[i // 2][2 + i % 2 : 3 + i % 2]
        weighted = new_weight.astype(BF16).astype(F32) * fresh_value
        for c in range(POSITIONS // CHUNK):
            weights = jnp.exp(s_ref[i, :, pl.ds(c * CHUNK, CHUNK)] - maximum)
            denominator = denominator + jnp.sum(weights, axis=1, keepdims=True)
            weighted = weighted + jnp.dot(
                weights.astype(BF16),
                v_ref[cache_rows[i], pl.ds(c * CHUNK, CHUNK), :],
                preferred_element_type=F32,
            )
        o_ref[pl.ds(first + i, GROUPED, stride=SLOTS), :] = weighted / denominator


def attend_near_kernel(limit_ref, m0, m1, k_ref, v_ref, o_ref, s_ref):
    o_ref[...] = jnp.zeros_like(o_ref)
    attend_pairs(0, (m0, m1), limit_ref, k_ref, v_ref, s_ref, o_ref)


def attend_next_kernel(limit_ref, before_ref, m2, k_ref, v_ref, o_ref, s_ref):
    o_ref[...] = before_ref[...]
    attend_pairs(4, (m2,), limit_ref, k_ref, v_ref, s_ref, o_ref)


def attend_far_kernel(limit_ref, before_ref, m0, m1, m2, m3, k_ref, v_ref, out_ref, s_ref, o_ref):
    o_ref[...] = before_ref[...]
    attend_pairs(6, (m3,), limit_ref, k_ref, v_ref, s_ref, o_ref)
    infos = [m[16:, :].astype(F32) for m in (m0, m1, m2, m3)]
    own_ids = jnp.concatenate([info[6:8] for info in infos], axis=0)
    core_ids = jnp.concatenate([infos[d ^ 1][8:10] for d in range(4)], axis=0)
    lanes = lax.broadcasted_iota(I32, (SLOTS, HEAD), 1)
    ids = jnp.where(lanes < HEAD // 2, own_ids, core_ids)
    block = jnp.concatenate(
        [o_ref[h * SLOTS : (h + 1) * SLOTS, :] for h in range(GROUPED)] + [ids], axis=1
    )
    pair = jnp.concatenate([block, block], axis=0).astype(BF16)
    for j in range(8):
        out_ref[j * 16 : (j + 1) * 16, :] = pair


def project_kernel(rows_ref, w_ref, w_core_ref, out_ref, place_ref):
    core = beam_index() & 1
    rows = rows_ref[:, :Q_COLS]
    sides = (core, 1 - core)
    for side, ref in zip(sides, (w_ref, w_core_ref)):
        terms = jnp.dot(rows, ref[...], preferred_element_type=F32).astype(BF16)
        for q in range(8):
            source = QUERY_ORDER.index(q) * 16
            at = jnp.where(side == 0, LINE_ORDER.index((q, 0)), LINE_ORDER.index((q, 1)))
            out_ref[pl.ds(pl.multiple_of(at * 16, 16), 16), :] = terms[source : source + 16]
    query = lax.axis_index("tensor")
    place = jnp.int32(0)
    for q in range(8):
        place = jnp.where(query == q, QUERY_ORDER.index(q), place)
    first = pl.multiple_of(place * 16, 16)
    lanes = lax.broadcasted_iota(I32, (16, HEAD), 1)
    ids = rows_ref[pl.ds(first, 16), Q_COLS:].astype(F32).astype(I32)
    for side, lane in zip(sides, (0, HEAD // 2)):
        place = (ids[:, lane : lane + 1] == lanes).astype(F32).astype(BF16)
        place_ref[pl.ds(pl.multiple_of(side * 16, 16), 16), :] = place


def finish_kernel(terms_ref, place_ref, out_ref):
    halves = []
    for core in range(2):
        total = jnp.zeros((16, 256), F32)
        for at, (_, source_core) in enumerate(LINE_ORDER):
            if source_core == core:
                total = total + terms_ref[at * 16 : at * 16 + 16, :].astype(F32)
        halves.append(total.astype(BF16))
    rows = jnp.concatenate(halves, axis=0)
    out_ref[...] = transposed_dot(place_ref[...], rows)[:BEAMS].astype(BF16)


def pack(parents, lengths, queries, token_keys, token_values):
    message = pltpu.VMEM((PACKED, HEAD), BF16)
    operands = (parents, lengths, queries, token_keys, token_values)
    return pl.pallas_call(
        pack_kernel,
        out_shape=(message,) * 4 + (pltpu.VMEM((SLOTS, HEAD), I32),),
        in_specs=[HBM] * 5,
        out_specs=(VMEM,) * 5,
        scratch_shapes=[
            pltpu.SMEM((SLOTS,), I32),
            pltpu.SMEM((SLOTS,), I32),
            pltpu.VMEM((SLOTS, Q_COLS), BF16),
            pltpu.VMEM((SLOTS, HEAD), BF16),
            pltpu.VMEM((SLOTS, HEAD), BF16),
            pltpu.VMEM((GROUPED * SLOTS, HEAD), F32),
            pltpu.VMEM((GROUPED * SLOTS, HEAD), F32),
            pltpu.VMEM((64, HEAD), F32),
            pltpu.SemaphoreType.DMA((5,)),
        ],
        compiler_params=pltpu.CompilerParams(vmem_limit_bytes=4 * MIB),
        cost_estimate=pl.CostEstimate(flops=2 * 10**10, bytes_accessed=0, transcendentals=0),
        name="pack",
    )(*[in_hbm(x) for x in operands])


def attend_early(kernel, slots, name, *operands):
    return pl.pallas_call(
        kernel,
        out_shape=jax.ShapeDtypeStruct((GROUPED * SLOTS, HEAD), F32),
        in_specs=[VMEM] * len(operands),
        out_specs=VMEM,
        scratch_shapes=[pltpu.VMEM((slots, GROUPED, POSITIONS), F32)],
        compiler_params=pltpu.CompilerParams(vmem_limit_bytes=16 * MIB),
        cost_estimate=pl.CostEstimate(flops=2 * 10**9, bytes_accessed=0, transcendentals=0),
        name=name,
    )(*operands)


def attend_far(*operands):
    return pl.pallas_call(
        attend_far_kernel,
        out_shape=jax.ShapeDtypeStruct((16 * SLOTS, OUT_COLS), BF16),
        in_specs=[VMEM] * len(operands),
        out_specs=VMEM,
        scratch_shapes=[
            pltpu.VMEM((2, GROUPED, POSITIONS), F32),
            pltpu.VMEM((GROUPED * SLOTS, HEAD), F32),
        ],
        compiler_params=pltpu.CompilerParams(vmem_limit_bytes=16 * MIB),
        name="attend_far",
    )(*operands)


def body(parents, lengths, queries, token_keys, token_values, key_cache, value_cache, weight):
    *messages, limits = pack(parents, lengths, queries, token_keys, token_values)
    arrived = [
        lax.ppermute(messages[d], BEAM_AXES, [(i, i ^ d) for i in range(32)]) for d in (1, 2, 3)
    ]
    caches = [x.reshape(SLOTS, POSITIONS, HEAD) for x in (key_cache, value_cache)]
    m0, m1, m2, m3 = [messages[0]] + arrived
    late_weight, m1 = lax.optimization_barrier((weight, m1))
    core_weight = lax.ppermute(late_weight, BEAM_AXES, [(i, i ^ 1) for i in range(32)])
    part = attend_early(attend_near_kernel, 4, "attend_near", limits, m0, m1, *caches)
    part = attend_early(attend_next_kernel, 2, "attend_next", limits, part, m2, *caches)
    heads = attend_far(limits, part, m0, m1, m2, m3, *caches)
    gathered = lax.all_to_all(heads, "beam", 0, 0, axis_index_groups=CHIP_GROUPS, tiled=True)
    terms, place = pl.pallas_call(
        project_kernel,
        out_shape=(pltpu.VMEM((256, 256), BF16), pltpu.VMEM((BEAMS, HEAD), BF16)),
        in_specs=[VMEM] * 3,
        out_specs=(VMEM, VMEM),
        compiler_params=pltpu.CompilerParams(vmem_limit_bytes=16 * MIB),
        name="project",
    )(gathered, weight, core_weight)
    shares = lax.all_to_all(
        terms, ("beam", "tensor"), 0, 0, axis_index_groups=LINE_GROUPS, tiled=True
    )
    return pl.pallas_call(
        finish_kernel,
        out_shape=jax.ShapeDtypeStruct((BEAMS, 256), BF16),
        in_specs=[VMEM] * 2,
        out_specs=VMEM,
        compiler_params=pltpu.CompilerParams(vmem_limit_bytes=16 * MIB),
        name="finish",
    )(shares, place)


def solution(mesh):
    in_specs = (
        P(BEAM_AXES),
        P(BEAM_AXES),
        P(BEAM_AXES, "tensor"),
        P(BEAM_AXES, "tensor"),
        P(BEAM_AXES, "tensor"),
        P(BEAM_AXES, "tensor", None, None),
        P(BEAM_AXES, "tensor", None, None),
        P("tensor", BEAM_AXES),
    )
    out_specs = P("tensor", BEAM_AXES)
    return jax.shard_map(body, mesh=mesh, in_specs=in_specs, out_specs=out_specs, check_vma=False)
```
